128 devices in a mesh: gx: 8 (over z, core), gy: 16 (over y, x).
Axes of the slice: x: 4, y: 4, z: 4, core: 2. Of those that a mesh axis runs over, the one named last changes fastest.
Arguments:
- block_vectors: bfloat16 [3, 128, 294912], P(None, None, ('gx', 'gy')), may hold values from -6 to 6
- connectivity: int32 [8, 294912], P(None, ('gx', 'gy')), may hold values from 0 to 2303
- density: float32 [294912], P(('gx', 'gy')), may hold values from 0.1 to 1
- stiff_factor: bfloat16 [24, 24], replicated, may hold values from -1.25 to 1.25
- mass_factor: bfloat16 [24, 24], replicated, may hold values from -1.25 to 1.25
- send_slot: int32 [128, 8, 96], P(('gx', 'gy')), may hold values from 0 to 2303, as said below
- send_count: int32 [128, 8], P(('gx', 'gy')), may hold values from 0 to 96, as said below
- recv_target: int32 [128, 8, 96], P(('gx', 'gy')), may hold values from 0 to 2303, as said below
- recv_weight: float32 [128, 8, 96], P(('gx', 'gy')), may hold values from 0.2 to 1
Outputs:
- filtered_density: float32 [294912], P(('gx', 'gy'))
- filtered_sens: float32 [294912], P(('gx', 'gy'))
- ritz_sum: float32 [], replicated
The draws below stay inside these ranges and needn't reach their ends.
Inputs may be any that keep to these rules, and one draw needn't show every extreme that they name: `send_slot`: a tile's live slots name distinct elements of the sender's rim layer, 2 elements deep, that faces the neighbour in that direction. `send_count`: 0 towards neighbours off the slab; otherwise at least three quarters of the facing rim layer on the four sides and at least half of it on the four corners; every device's tile to the next device along gy (the last one's: to the previous) is full. `recv_target`: elements of the owner's rim layer, 2 elements deep, that faces the sender.
All inputs are finite; a program needn't handle non-finite values.
Results may differ from the reference program's by a relative error of at most 0.0011.
Values sent between devices are 32-bit elements; how exact they have to be, the bound alone decides.
No kernel may reach another device: no remote copies, remote signals or barrier semaphores. Data moves between devices by JAX's collectives and lax.ppermute only.
A program may use at most 64 MiB of HBM per device.

```python
import jax
import jax.numpy as jnp
from jax import lax

NV = 128
SIDE = 48
RADIUS = 2
ELEMS_DEV = 2304
NODES_DEV = 2304
CAP = 96
GRID_ROWS = 8
GRID_COLS = 16
PEERS = 128
ELEMS = 294912
NODES = 294912


DIRECTIONS = ((-1, -1), (-1, 0), (-1, 1), (0, -1), (0, 1), (1, -1), (1, 0), (1, 1))


def layer_shape(direction):
    step_row, step_col = direction
    row_len = RADIUS if step_row != 0 else SIDE
    col_len = RADIUS if step_col != 0 else SIDE
    row_start = SIDE - RADIUS if step_row == 1 else 0
    col_start = SIDE - RADIUS if step_col == 1 else 0
    return (row_len, col_len, row_start, col_start)


def element_layer_entry(direction, picks):
    row_len, col_len, row_start, col_start = layer_shape(direction)
    picks = picks % (row_len * col_len)
    return (row_start + picks // col_len) * SIDE + col_start + picks % col_len


def draw_send_slot(key, part):
    tables = []
    for position, direction in enumerate(DIRECTIONS):
        row_len, col_len, row_start, col_start = layer_shape(direction)
        layer = row_len * col_len
        scores = jax.random.randint(jax.random.fold_in(key, 11 + position), (PEERS, CAP), 0, 1 << 14)
        slots = jax.lax.broadcasted_iota(jnp.int32, (PEERS, CAP), 1)
        scores = jnp.where(slots < layer, scores, 1 << 14) * CAP + slots
        order = jnp.argsort(scores, axis=1).astype(jnp.int32)
        tables.append(element_layer_entry(direction, order))
    return jnp.stack(tables, axis=1).astype(jnp.int32)


def draw_send_count(key, part):
    peer_ids = jax.lax.broadcasted_iota(jnp.int32, (PEERS,), 0)
    row_of = peer_ids // GRID_COLS
    col_of = peer_ids % GRID_COLS
    columns = []
    for position, direction in enumerate(DIRECTIONS):
        step_row, step_col = direction
        row_len, col_len, row_start, col_start = layer_shape(direction)
        layer = row_len * col_len
        lowest = 3 * layer // 4 if step_row == 0 or step_col == 0 else layer // 2
        drawn = jax.random.randint(jax.random.fold_in(key, 31 + position), (PEERS,), lowest, layer + 1)
        if direction == (0, 1):
            drawn = jnp.where(col_of < GRID_COLS - 1, layer, drawn)
        if direction == (0, -1):
            drawn = jnp.where(col_of == GRID_COLS - 1, layer, drawn)
        there = (row_of + step_row >= 0) & (row_of + step_row < GRID_ROWS) & (col_of + step_col >= 0) & (col_of + step_col < GRID_COLS)
        columns.append(jnp.where(there, drawn, 0))
    return jnp.stack(columns, axis=1).astype(jnp.int32)


def draw_recv_target(key, part):
    tables = []
    for position, direction in enumerate(DIRECTIONS):
        facing = (-direction[0], -direction[1])
        row_len, col_len, row_start, col_start = layer_shape(facing)
        picks = jax.random.randint(jax.random.fold_in(key, 51 + position), (PEERS, CAP), 0, row_len * col_len)
        tables.append(element_layer_entry(facing, picks))
    return jnp.stack(tables, axis=1).astype(jnp.int32)


def plant(values, key, low, largest):
    place = [jax.random.randint(jax.random.fold_in(key, axis), (), 0, length) for axis, length in enumerate(values.shape)]
    main_axis = values.shape.index(max(values.shape))
    next_to = place[:main_axis] + [(place[main_axis] + 1) % values.shape[main_axis]] + place[main_axis + 1:]
    return values.at[tuple(place)].set(low).at[tuple(next_to)].set(largest)


def block_levels(own_key, extent, pieces, least, top_value):
    factor_of = 1.0
    for axis_at, shards_of in pieces:
        draws = jax.random.uniform(jax.random.fold_in(jax.random.fold_in(own_key, 6), axis_at), (shards_of,), jnp.float32, least / len(pieces), top_value / len(pieces))
        factor_of = factor_of * jnp.repeat(jnp.exp(draws), extent[axis_at] // shards_of).reshape((-1,) + (1,) * (len(extent) - 1 - axis_at))
    return factor_of


def normal_values(stream_key, shape, deviation, bound, pieces=(), kind=jnp.bfloat16):
    values = deviation * jax.random.normal(stream_key, shape, jnp.float32)
    if pieces:
        values = values * block_levels(stream_key, shape, pieces, -0.22, 0.18)
    return jnp.clip(values, -bound, bound).astype(kind)


def setup_inputs(seed: int = 0) -> dict:
    keys = jax.random.split(jax.random.key(seed), 10)
    return {
        "block_vectors": normal_values(keys[0], (3, NV, NODES), 1.0, 6.0, ((2, 128),)),
        "connectivity": plant(jax.random.randint(keys[1], (8, ELEMS), 0, NODES_DEV), jax.random.fold_in(keys[1], 1), 0, NODES_DEV - 1).astype(jnp.int32),
        "density": jnp.clip(0.1 + 0.9 * jax.random.uniform(keys[2], (ELEMS,), jnp.float32) ** block_levels(keys[2], (ELEMS,), ((0, 128),), -0.2, 0.2), 0.1, 1.0),
        "stiff_factor": normal_values(keys[3], (24, 24), 24 ** -0.5, 1.25),
        "mass_factor": normal_values(keys[4], (24, 24), 24 ** -0.5, 1.25),
        "send_slot": draw_send_slot(jax.random.fold_in(keys[9], 71), 0),
        "send_count": draw_send_count(jax.random.fold_in(keys[9], 71), 0),
        "recv_target": draw_recv_target(jax.random.fold_in(keys[9], 71), 0),
        "recv_weight": jnp.clip(0.2 + 0.8 * jax.random.uniform(keys[8], (PEERS, 8, CAP), jnp.float32) ** block_levels(keys[8], (PEERS, 8, CAP), ((0, 128),), -0.2, 0.2), 0.2, 1.0),
    }


DIRECTIONS = ((-1, -1), (-1, 0), (-1, 1), (0, -1), (0, 1), (1, -1), (1, 0), (1, 1))

def invert_spd(gram, vec_count):
    factor_low = jnp.linalg.cholesky(gram)
    eye = jnp.eye(vec_count, dtype=gram.dtype)
    lower_inv = lax.linalg.triangular_solve(factor_low, eye, left_side=True, lower=True)
    return lax.linalg.triangular_solve(factor_low, lower_inv, left_side=True, lower=True, transpose_a=True)

def project(vec_one, conn_one, factors, vec_count):
    width = conn_one.shape[1]
    picked = vec_one[:, :, conn_one]
    picked = jnp.transpose(picked, (0, 2, 1, 3)).reshape(24, vec_count * width)
    projected = jnp.dot(factors.astype(jnp.float32), picked.astype(jnp.float32), preferred_element_type=jnp.float32).astype(jnp.bfloat16)
    return projected.reshape(48, vec_count, width)

def reference(block_vectors, connectivity, density, stiff_factor, mass_factor, send_slot, send_count, recv_target, recv_weight):
    highest_precision = lax.Precision.HIGHEST
    factors = jnp.concatenate([stiff_factor, mass_factor], axis=0)
    vec_dev = block_vectors.reshape(3, NV, PEERS, NODES_DEV).transpose(2, 0, 1, 3)
    conn_dev = connectivity.reshape(8, PEERS, ELEMS_DEV).transpose(1, 0, 2)
    dens_dev = density.reshape(PEERS, ELEMS_DEV)

    def gram_step(totals, item):
        vec_one, conn_one, dens_one = item
        projected = project(vec_one, conn_one, factors, NV)
        proj_stiff = projected[:24].astype(jnp.float32)
        projected_mass_matrix = projected[24:].astype(jnp.float32)
        weighted_stiff = lax.optimization_barrier((proj_stiff * (dens_one ** 3)[None, None, :]).astype(jnp.bfloat16)).astype(jnp.float32)
        weighted_mass = lax.optimization_barrier((projected_mass_matrix * dens_one[None, None, :]).astype(jnp.bfloat16)).astype(jnp.float32)
        part_stiff = jnp.einsum('ivb,iwb->vw', weighted_stiff, proj_stiff, precision=highest_precision)
        part_mass = jnp.einsum('ivb,iwb->vw', weighted_mass, projected_mass_matrix, precision=highest_precision)
        return ((totals[0] + part_stiff, totals[1] + part_mass), None)
    zero_gram = jnp.zeros((NV, NV), jnp.float32)
    (stiffness_gram_matrix, gram_mass), _ = lax.scan(gram_step, (zero_gram, zero_gram), (vec_dev, conn_dev, dens_dev))
    stiffness_gram_matrix = 0.5 * (stiffness_gram_matrix + stiffness_gram_matrix.T)
    gram_mass = 0.5 * (gram_mass + gram_mass.T)
    inv_mass = invert_spd(gram_mass, NV)
    sandwich_product = jnp.dot(jnp.dot(inv_mass, stiffness_gram_matrix, precision=highest_precision), inv_mass, precision=highest_precision)
    ritz_sum = jnp.sum(inv_mass * stiffness_gram_matrix) / NV
    inv_round = lax.optimization_barrier(inv_mass.astype(jnp.bfloat16)).astype(jnp.float32)
    sandwich_rounding = lax.optimization_barrier(sandwich_product.astype(jnp.bfloat16)).astype(jnp.float32)

    def energy_step(unused, item):
        vec_one, conn_one, dens_one = item
        projected = project(vec_one, conn_one, factors, NV)
        proj_stiff = projected[:24].astype(jnp.float32)
        projected_mass_matrix = projected[24:].astype(jnp.float32)
        inner_stiff = jnp.einsum('fc,hca->hfa', inv_round, proj_stiff, precision=highest_precision)
        inner_mass_product = jnp.einsum('fc,hca->hfa', sandwich_rounding, projected_mass_matrix, precision=highest_precision)
        energy_stiff = jnp.sum(inner_stiff * proj_stiff, axis=(0, 1))
        energy_mass = jnp.sum(inner_mass_product * projected_mass_matrix, axis=(0, 1))
        sens_one = ELEMS / NV * (3.0 * dens_one * dens_one * energy_stiff - energy_mass)
        return (unused, sens_one)
    _, sens_dev = lax.scan(energy_step, jnp.zeros((), jnp.float32), (vec_dev, conn_dev, dens_dev))
    slot_flat = send_slot.reshape(PEERS, 8 * CAP).astype(jnp.int32)
    tile_density = jnp.take_along_axis(dens_dev, slot_flat, axis=1).reshape(PEERS, 8, CAP)
    tile_sens = jnp.take_along_axis(sens_dev, slot_flat, axis=1).reshape(PEERS, 8, CAP)
    live_out = lax.broadcasted_iota(jnp.int32, (PEERS, 8, CAP), 2) < send_count[:, :, None]
    tile_density = jnp.where(live_out, tile_density, 0.0)
    tile_sens = jnp.where(live_out, tile_sens, 0.0)
    peer_ids = jnp.arange(PEERS, dtype=jnp.int32)
    row_of = peer_ids // GRID_COLS
    col_of = peer_ids % GRID_COLS
    parts_density, parts_sens, parts_count = ([], [], [])
    for position, (step_row, step_col) in enumerate(DIRECTIONS):
        src_row = row_of - step_row
        src_col = col_of - step_col
        valid = (src_row >= 0) & (src_row < GRID_ROWS) & (src_col >= 0) & (src_col < GRID_COLS)
        source = (jnp.clip(src_row, 0, GRID_ROWS - 1) * GRID_COLS + jnp.clip(src_col, 0, GRID_COLS - 1)).astype(jnp.int32)
        parts_density.append(jnp.where(valid[:, None], tile_density[source, position], 0.0))
        parts_sens.append(jnp.where(valid[:, None], tile_sens[source, position], 0.0))
        parts_count.append(jnp.where(valid, send_count[source, position], 0).astype(jnp.int32))
    recv_density = jnp.stack(parts_density, axis=1)
    recv_sens = jnp.stack(parts_sens, axis=1)
    recv_count = jnp.stack(parts_count, axis=1)

    def owner_sum(rdens, rsens, rcount, targets, weights):
        live_in = lax.broadcasted_iota(jnp.int32, (8, CAP), 1) < rcount[:, None]
        live_weight = jnp.where(live_in, weights, 0.0)
        stacked = jnp.stack([live_weight, live_weight * rdens, live_weight * rsens], axis=-1).reshape(8 * CAP, 3)
        return jax.ops.segment_sum(stacked, targets.reshape(8 * CAP), num_segments=ELEMS_DEV)
    sums = jax.vmap(owner_sum)(recv_density, recv_sens, recv_count, recv_target, recv_weight)
    denominator = 1.0 + sums[:, :, 0]
    filtered_density = ((dens_dev + sums[:, :, 1]) / denominator).reshape(ELEMS)
    filtered_sens = ((sens_dev + sums[:, :, 2]) / denominator).reshape(ELEMS)
    return (filtered_density, filtered_sens, ritz_sum)
```

```python
import jax
import jax.numpy as jnp
from jax import lax
from jax.experimental import pallas as pl
from jax.experimental.pallas import tpu as pltpu
from jax.sharding import PartitionSpec as P

SIDE = 48
RIM = 2
LANES = 128
GROUP = 8
UNIT = 32
ROWS = 24 * GROUP
AXES = ("gx", "gy")
VMEM_LIMIT = 60 * 1024 * 1024
F32 = jnp.float32
BF16 = jnp.bfloat16
HIGHEST = lax.Precision.HIGHEST


def iota(shape, dim):
    return lax.broadcasted_iota(jnp.int32, shape, dim)


def density_columns(dens_ref, dcol):
    for j in range(dens_ref.shape[0]):
        row = jnp.broadcast_to(dens_ref[j : j + 1, :], (LANES, LANES))
        dcol[pl.ds(j * LANES, LANES), :] = row.T


PIECES = (
    ((0, 0), (1, 3), (2, 6)),
    ((2, -2), (3, 1), (4, 4), (5, 7)),
    ((5, -1), (6, 2), (7, 5)),
)


def gram_kernel(
    elems, per_step, conn_ref, vec_ref, dens_ref, w_ref, p_ref, out_ref, table, dcol, x_even, x_odd, weighted, acc
):
    step = pl.program_id(0)
    units = elems // UNIT
    sub = iota((8, LANES), 0)

    def gather(unit, xbuf):
        base = unit * UNIT
        for q in range(UNIT // 16):
            for h in range(2):
                for pair in range(4):
                    regs = []
                    for e in range(2):
                        at = base + (q * 16 + h * 8 + pair * 2 + e)
                        rows = [conn_ref[a * elems + at] for a in range(8)]
                        for pieces in PIECES:
                            value = None
                            for corner, first in pieces:
                                got = table[pl.ds(rows[corner] + (8 - first), 8), :]
                                value = got if value is None else jnp.where(sub >= first, got, value)
                            regs.append(value)
                    block = jnp.concatenate(regs, axis=0).astype(BF16)
                    xbuf[q, pl.ds(pair * 48, 48), pl.ds(h * LANES, LANES)] = block

    @pl.when(step == 0)
    def _():
        for c in range(3):
            for j in range(elems // LANES):
                block = vec_ref[c, :, pl.ds(j * LANES, LANES)].astype(F32).T
                table[pl.ds(8 + 3 * LANES * j + c, LANES, stride=3), :] = block
        density_columns(dens_ref, dcol)
        acc[...] = jnp.zeros_like(acc)
        gather(0, x_even)

    def compute(unit, local, xbuf):
        for q in range(UNIT // 16):
            full = jnp.dot(w_ref[...], xbuf[q], preferred_element_type=F32).astype(BF16)
            for h in range(2):
                part = full[:, h * LANES : (h + 1) * LANES]
                chunk = 2 * q + h
                p_ref[local * 4 + chunk] = part
                wide = part.astype(F32).reshape(2, 24, 8, LANES)
                dens = dcol[pl.ds(pl.multiple_of(unit * UNIT + chunk * 8, 8), 8), :]
                weighted[0, chunk] = (wide[0] * (dens * dens * dens)[None]).reshape(ROWS, LANES).astype(BF16)
                weighted[1, chunk] = (wide[1] * dens[None]).reshape(ROWS, LANES).astype(BF16)
        for kind in range(2):
            left = weighted[kind].reshape(4 * ROWS, LANES)
            right = p_ref[pl.ds(local * 4, 4), pl.ds(kind * ROWS, ROWS), :].reshape(4 * ROWS, LANES)
            acc[kind] += lax.dot_general(left, right, (((0,), (0,)), ((), ())), preferred_element_type=F32)

    def body(it, _):
        unit = step * per_step + 2 * it
        gather(unit + 1, x_odd)
        compute(unit, 2 * it, x_even)
        gather(jnp.minimum(unit + 2, units - 1), x_even)
        compute(unit + 1, 2 * it + 1, x_odd)
        return 0

    lax.fori_loop(0, per_step // 2, body, 0)

    @pl.when(step == pl.num_programs(0) - 1)
    def _():
        stiff = 0.5 * (acc[0] + acc[0].T)
        mass = 0.5 * (acc[1] + acc[1].T)
        row, col = iota((LANES, LANES), 0), iota((LANES, LANES), 1)
        out_ref[0:LANES, :] = jnp.where(row <= col, stiff, mass)
        diag = jnp.sum(jnp.where(row == col, mass, 0.0), axis=0, keepdims=True)
        out_ref[LANES : LANES + 8, :] = jnp.broadcast_to(diag, (8, LANES))


def invert_spd(gram):
    lane = iota((8, LANES), 1)
    sub = iota((8, LANES), 0)
    regs = [gram[8 * g : 8 * g + 8, :] for g in range(16)]
    for k in range(LANES):
        own, at = k // 8, k % 8
        row = regs[own][at : at + 1, :]
        inverse = 1.0 / row[:, k : k + 1]
        row = jnp.where(lane[:1] == k, inverse, row * inverse)
        row = jnp.broadcast_to(row, (8, LANES))
        here = lane == k
        for g in range(16):
            col = jnp.broadcast_to(regs[g][:, k : k + 1], (8, LANES))
            new = jnp.where(here, 0.0, regs[g]) - col * row
            regs[g] = jnp.where(sub == at, row, new) if g == own else new
    return jnp.concatenate(regs, axis=0)


def rims(column, scale):
    elems = column.shape[0]

    def summed(rows):
        return jnp.sum(rows.T, axis=0, keepdims=True) * scale

    def side(first):
        parts = [column[pl.ds(first + c, SIDE, stride=SIDE), :] for c in range(RIM)]
        parts.append(jnp.zeros((LANES - RIM * SIDE, LANES), F32))
        return summed(jnp.concatenate(parts, axis=0))

    top = summed(column[pl.ds(0, LANES), :])
    bottom = summed(column[pl.ds(elems - LANES, LANES), :])
    left, right = side(0), side(SIDE - RIM)
    return jnp.concatenate([top, top, top, left, right, bottom, bottom, bottom], axis=0)


def energy_kernel(
    scale, gram_ref, p_hbm, dens_ref, slot_ref, live_ref, sens_ref, tile_ref, ritz_ref, p_vmem, dcol, both, total, sems
):
    elems = dcol.shape[0]
    groups = elems // GROUP
    pieces = sems.shape[0]
    span = groups // pieces
    copies = [
        pltpu.make_async_copy(
            p_hbm.at[pl.ds(i * span, span)], p_vmem.at[pl.ds(i * span, span)], sems.at[i]
        )
        for i in range(pieces)
    ]
    for copy in copies:
        copy.start()
    density_columns(dens_ref, dcol)
    slots = slot_ref[...]
    live = live_ref[...]
    tile_dens = jnp.take_along_axis(rims(dcol, 1.0 / LANES), slots, axis=1) * live

    row, col = iota((LANES, LANES), 0), iota((LANES, LANES), 1)
    packed = gram_ref[0:LANES, :]
    above = jnp.where(row < col, packed, 0.0)
    below = jnp.where(row > col, packed, 0.0)
    stiff = above + above.T + jnp.where(row == col, packed, 0.0)
    mass = below + below.T + jnp.where(row == col, gram_ref[LANES : LANES + 1, :], 0.0)
    inv_mass = invert_spd(mass)
    ritz_ref[0, 0] = jnp.sum(inv_mass * stiff) * (1.0 / LANES)
    half = jnp.dot(inv_mass, stiff, precision=HIGHEST, preferred_element_type=F32)
    sandwich = jnp.dot(half, inv_mass, precision=HIGHEST, preferred_element_type=F32)
    both[...] = jnp.zeros_like(both)
    both[0:LANES, 0:LANES] = inv_mass.astype(BF16)
    both[LANES:, LANES:] = sandwich.astype(BF16)

    per_piece = span * GROUP // UNIT
    for i in range(pieces):
        copies[i].wait()

        def body(it, _, i=i):
            unit = i * per_piece + it
            stiffs = p_vmem[pl.ds(unit * 4, 4), 0:ROWS, :].reshape(4 * ROWS, LANES)
            masses = p_vmem[pl.ds(unit * 4, 4), ROWS:, :].reshape(4 * ROWS, LANES)
            inner = jnp.dot(
                jnp.concatenate([stiffs, masses], axis=1), both[...], preferred_element_type=F32
            )
            part_stiff = (inner[:, :LANES] * stiffs.astype(F32)).reshape(4, 24, 8, LANES).sum(axis=1)
            part_mass = (inner[:, LANES:] * masses.astype(F32)).reshape(4, 24, 8, LANES).sum(axis=1)
            at = pl.ds(pl.multiple_of(unit * UNIT, UNIT), UNIT)
            dens = dcol[at, :]
            total[at, :] = 3.0 * dens * dens * part_stiff.reshape(UNIT, LANES) - part_mass.reshape(UNIT, LANES)
            return 0

        lax.fori_loop(0, per_piece, body, 0)

    for j in range(elems // LANES):
        block = total[pl.ds(j * LANES, LANES), :]
        sens_ref[j : j + 1, :] = jnp.sum(block.T, axis=0, keepdims=True) * scale
    tile_sens = jnp.take_along_axis(rims(total, scale), slots, axis=1) * live
    tile_ref[...] = jnp.zeros_like(tile_ref)
    for ch, value in enumerate((live, tile_dens, tile_sens)):
        tile_ref[0, 3 * ch : 3 * ch + 3, :] = value[0:3]
        tile_ref[1, 3 * ch : 3 * ch + 3, :] = value[5:8]
        tile_ref[2, ch : ch + 1, :] = value[3:4]
        tile_ref[3, ch : ch + 1, :] = value[4:5]


def split3(value):
    high = value.astype(BF16)
    rest = value - high.astype(F32)
    mid = rest.astype(BF16)
    low = (rest - mid.astype(F32)).astype(BF16)
    return high, mid, low


def owner_kernel(up_ref, down_ref, left_ref, right_ref, target_ref, weight_ref, dens_ref, sens_ref, fdens_ref, fsens_ref):
    lane = iota((1, LANES), 1)

    def lanes_of(main, corner):
        return jnp.where(lane < 96, main, pltpu.roll(corner, 96, 1))

    values = [[], [], []]
    for ch in range(3):
        up = up_ref[3 * ch + 1 : 3 * ch + 2, :]
        down = down_ref[3 * ch + 1 : 3 * ch + 2, :]
        left = left_ref[3 * ch : 3 * ch + 3, :]
        right = right_ref[3 * ch : 3 * ch + 3, :]
        sides = (
            lanes_of(up, left[1:2]),
            lanes_of(down, left[2:3]),
            lanes_of(left[0:1], right[1:2]),
            lanes_of(right[0:1], right[2:3]),
        )
        for side in range(4):
            values[ch].append(sides[side] * weight_ref[side : side + 1, :])
    stacked = jnp.concatenate([jnp.concatenate(v, axis=1) for v in values], axis=0)
    high, mid, low = split3(stacked)
    left = jnp.concatenate([high, mid, low, jnp.zeros((7, 4 * LANES), BF16)], axis=0)
    targets = jnp.concatenate([target_ref[i : i + 1, :] for i in range(4)], axis=1)
    for j in range(dens_ref.shape[0]):
        hit = targets == iota((LANES, 4 * LANES), 0) + j * LANES
        hot = jnp.where(hit, 1.0, 0.0).astype(BF16)
        sums = lax.dot_general(left, hot, (((1,), (1,)), ((), ())), preferred_element_type=F32)
        sums = sums[0:3] + sums[3:6] + sums[6:9]
        under = 1.0 + sums[0:1]
        fdens_ref[j : j + 1, :] = (dens_ref[j : j + 1, :] + sums[1:2]) / under
        fsens_ref[j : j + 1, :] = (sens_ref[j : j + 1, :] + sums[2:3]) / under


def place(index, sizes):
    rows, cols = sizes
    return [index // cols // 2, index // cols % 2, index % cols // 4, index % 4]


def swapped(sizes, axis, step):
    rows, cols = sizes
    lengths = [rows // 2, 2, cols // 4, 4]
    pairs = []
    for i in range(rows * cols):
        at = place(i, sizes)
        at[axis] = (at[axis] + step) % lengths[axis]
        pairs.append((i, ((at[0] * 2 + at[1]) * lengths[2] + at[2]) * 4 + at[3]))
    return pairs


def sum_over_devices(value, sizes):
    value = value + lax.ppermute(value, AXES, swapped(sizes, 1, 1))
    lengths = [sizes[0] // 2, 2, sizes[1] // 4, 4]
    for axis in (3, 2, 0):
        others = [lax.ppermute(value, AXES, swapped(sizes, axis, s)) for s in range(1, lengths[axis])]
        for other in others:
            value = value + other
    return value


def torus(axis, step):
    size = lax.axis_size(axis)
    return [(i, (i + step) % size) for i in range(size)]


def per_device(
    block_vectors, connectivity, density, stiff_factor, mass_factor, send_slot, send_count, recv_target, recv_weight
):
    vec_count = block_vectors.shape[1]
    elems = density.shape[0]
    groups = elems // GROUP
    sizes = (lax.axis_size("gx"), lax.axis_size("gy"))
    scale = float(elems * sizes[0] * sizes[1]) / vec_count

    factors = jnp.stack([stiff_factor, mass_factor]).reshape(2, 24, 3, 8).transpose(0, 1, 3, 2).reshape(48, 24)
    eye = jnp.eye(GROUP, dtype=BF16)
    spread = (factors[:, None, None, :] * eye[None, :, :, None]).reshape(48 * GROUP, ROWS)
    conn_rows = (connectivity * 3).reshape(8 * elems)
    dens_rows = density.reshape(elems // LANES, LANES)

    steps = 9
    per_step = elems // UNIT // steps
    vmem = pl.BlockSpec(memory_space=pltpu.VMEM)
    smem = pl.BlockSpec(memory_space=pltpu.SMEM)
    proj, gram = pl.pallas_call(
        lambda *refs: gram_kernel(elems, per_step, *refs),
        grid=(steps,),
        out_shape=(
            jax.ShapeDtypeStruct((groups, 2 * ROWS, LANES), BF16),
            jax.ShapeDtypeStruct((LANES + 8, LANES), F32),
        ),
        in_specs=[smem, vmem, vmem, vmem],
        out_specs=(
            pl.BlockSpec((groups // steps, 2 * ROWS, LANES), lambda i: (i, 0, 0)),
            pl.BlockSpec((LANES + 8, LANES), lambda i: (0, 0)),
        ),
        scratch_shapes=[
            pltpu.VMEM((3 * elems + 24, LANES), F32),
            pltpu.VMEM((elems, LANES), F32),
            pltpu.VMEM((UNIT // 16, ROWS, 2 * LANES), BF16),
            pltpu.VMEM((UNIT // 16, ROWS, 2 * LANES), BF16),
            pltpu.VMEM((2, UNIT // GROUP, ROWS, LANES), BF16),
            pltpu.VMEM((2, LANES, LANES), F32),
        ],
        compiler_params=pltpu.CompilerParams(vmem_limit_bytes=VMEM_LIMIT),
        name="gram",
    )(conn_rows, block_vectors, dens_rows, spread)

    gram = sum_over_devices(gram, sizes)

    slots = send_slot[0]
    live = iota(slots.shape, 1) < send_count[0][:, None]
    row, col = slots // SIDE, slots % SIDE
    k = iota(slots.shape, 0)
    rim_place = jnp.where(
        k < 3,
        slots,
        jnp.where(
            k == 3,
            col * SIDE + row,
            jnp.where(k == 4, (col - (SIDE - RIM)) * SIDE + row, slots - (elems - LANES)),
        ),
    )
    pad = ((0, 0), (0, LANES - slots.shape[1]))
    rim_place = jnp.pad(jnp.where(live, rim_place, 0), pad)
    live = jnp.pad(live.astype(F32), pad)

    sens_rows, tiles, ritz = pl.pallas_call(
        lambda *refs: energy_kernel(scale, *refs),
        out_shape=(
            jax.ShapeDtypeStruct((elems // LANES, LANES), F32),
            jax.ShapeDtypeStruct((4, 16, LANES), F32),
            jax.ShapeDtypeStruct((1, 1), F32),
        ),
        in_specs=[vmem, pl.BlockSpec(memory_space=pl.ANY), vmem, vmem, vmem],
        out_specs=(vmem, vmem, smem),
        scratch_shapes=[
            pltpu.VMEM((groups, 2 * ROWS, LANES), BF16),
            pltpu.VMEM((elems, LANES), F32),
            pltpu.VMEM((2 * LANES, 2 * LANES), BF16),
            pltpu.VMEM((elems, LANES), F32),
            pltpu.SemaphoreType.DMA((6,)),
        ],
        compiler_params=pltpu.CompilerParams(vmem_limit_bytes=VMEM_LIMIT),
        name="energy",
    )(gram, proj, dens_rows, rim_place, live)

    up = lax.ppermute(tiles[0], "gx", torus("gx", -1))
    down = lax.ppermute(tiles[1], "gx", torus("gx", 1))
    to_left = jnp.stack([tiles[2, 0:3], up[0:9:3], down[0:9:3]], axis=1).reshape(9, LANES)
    to_right = jnp.stack([tiles[3, 0:3], up[2:9:3], down[2:9:3]], axis=1).reshape(9, LANES)
    left = lax.ppermute(to_left, "gy", torus("gy", -1))
    right = lax.ppermute(to_right, "gy", torus("gy", 1))

    def by_side(table):
        corner = LANES - table.shape[2]
        rows = [table[0, main : main + 1] for main in (1, 6, 3, 4)]
        ends = [table[0, k : k + 1, :corner] for k in (0, 5, 2, 7)]
        return jnp.concatenate(
            [jnp.concatenate(rows, axis=0), jnp.concatenate(ends, axis=0)], axis=1
        )

    fdens, fsens = pl.pallas_call(
        owner_kernel,
        out_shape=(jax.ShapeDtypeStruct((elems // LANES, LANES), F32),) * 2,
        in_specs=[vmem] * 8,
        out_specs=(vmem, vmem),
        name="owner",
    )(up, down, left, right, by_side(recv_target), by_side(recv_weight), dens_rows, sens_rows)
    return fdens.reshape(elems), fsens.reshape(elems), ritz.reshape(())


def solution(mesh):
    placed = (
        P(None, None, ("gx", "gy")),
        P(None, ("gx", "gy")),
        P(("gx", "gy")),
        P(),
        P(),
        P(("gx", "gy"), None, None),
        P(("gx", "gy"), None),
        P(("gx", "gy"), None, None),
        P(("gx", "gy"), None, None),
    )
    return jax.shard_map(
        per_device,
        mesh=mesh,
        in_specs=placed,
        out_specs=(P(("gx", "gy")), P(("gx", "gy")), P()),
        check_vma=False,
    )
```

```python
import jax
import jax.numpy as jnp
from jax import lax
from jax.experimental import pallas as pl
from jax.experimental.pallas import tpu as pltpu
from jax.sharding import PartitionSpec as P

SIDE = 48
RIM = 2
LANES = 128
GROUP = 8
UNIT = 32
ROWS = 24 * GROUP
AXES = ("gx", "gy")
VMEM_LIMIT = 60 * 1024 * 1024
F32 = jnp.float32
BF16 = jnp.bfloat16
HIGHEST = lax.Precision.HIGHEST


def iota(shape, dim):
    return lax.broadcasted_iota(jnp.int32, shape, dim)


def density_columns(dens_ref, dcol):
    for j in range(dens_ref.shape[0]):
        row = jnp.broadcast_to(dens_ref[j : j + 1, :], (LANES, LANES))
        dcol[pl.ds(j * LANES, LANES), :] = row.T


PIECES = (
    ((0, 0), (1, 3), (2, 6)),
    ((2, -2), (3, 1), (4, 4), (5, 7)),
    ((5, -1), (6, 2), (7, 5)),
)


def spread(factor):
    dofs = factor.shape[0]
    wide, tall = (ROWS, dofs), (dofs, ROWS)
    take_row = (iota(wide, 0) >> 3) == iota(wide, 1)
    out = iota(tall, 1)
    within = lax.rem(out, dofs)
    corner = within // 3
    take_col = (within - 3 * corner) * 8 + corner == iota(tall, 0)
    picked = jnp.dot(jnp.where(take_row, 1.0, 0.0).astype(BF16), factor, preferred_element_type=F32)
    full = jnp.dot(picked.astype(BF16), jnp.where(take_col, 1.0, 0.0).astype(BF16), preferred_element_type=F32)
    square = (ROWS, ROWS)
    same = (iota(square, 0) & 7) == iota(square, 1) // dofs
    return jnp.where(same, full, 0.0).astype(BF16)


def gram_kernel(
    elems, per_step, conn_ref, vec_ref, dens_ref, stiff_ref, mass_ref, p_ref, out_ref,
    table, dcol, w_ref, tripled, rows_smem, x_even, x_odd, k_even, k_odd, acc, sem
):
    step = pl.program_id(0)
    units = elems // UNIT
    sub = iota((8, LANES), 0)

    def gather(unit, xbuf, qs=tuple(range(UNIT // 16))):
        base = unit * UNIT
        for q in qs:
            for h in range(2):
                for pair in range(4):
                    regs = []
                    for e in range(2):
                        at = base + (q * 16 + h * 8 + pair * 2 + e)
                        rows = [rows_smem[a * elems + at] for a in range(8)]
                        for pieces in PIECES:
                            value = None
                            for corner, first in pieces:
                                got = table[pl.ds(rows[corner] + (8 - first), 8), :]
                                value = got if value is None else jnp.where(sub >= first, got, value)
                            regs.append(value)
                    block = jnp.concatenate(regs, axis=0).astype(BF16)
                    xbuf[q, pl.ds(pair * 48, 48), pl.ds(h * LANES, LANES)] = block

    @pl.when(step == 0)
    def _():
        tripled[...] = conn_ref[...] * 3
        copies = [
            pltpu.make_async_copy(tripled.at[a], rows_smem.at[pl.ds(a * elems, elems)], sem.at[a]) for a in range(8)
        ]
        for copy in copies:
            copy.start()
        w_ref[0:ROWS] = spread(stiff_ref[...])
        w_ref[ROWS:] = spread(mass_ref[...])
        for c in range(3):
            for j in range(elems // LANES):
                block = vec_ref[c, :, pl.ds(j * LANES, LANES)].astype(F32).T
                table[pl.ds(8 + 3 * LANES * j + c, LANES, stride=3), :] = block
        density_columns(dens_ref, dcol)
        acc[...] = jnp.zeros_like(acc)
        k_odd[...] = jnp.zeros_like(k_odd)
        for copy in copies:
            copy.wait()
        gather(0, x_even)

    def project(unit, local, xbuf, kept, qs):
        for q in qs:
            full = jnp.dot(w_ref[...], xbuf[q], preferred_element_type=F32).astype(BF16)
            for h in range(2):
                part = full[:, h * LANES : (h + 1) * LANES]
                chunk = 2 * q + h
                p_ref[local * 4 + chunk] = part
                wide = part.astype(F32).reshape(2, 24, 8, LANES)
                dens = dcol[pl.ds(pl.multiple_of(unit * UNIT + chunk * 8, 8), 8), :]
                for kind, factor in enumerate((dens * dens * dens, dens)):
                    kept[kind, chunk] = part[kind * ROWS : (kind + 1) * ROWS]
                    kept[2 + kind, chunk] = (wide[kind] * factor[None]).reshape(ROWS, LANES).astype(BF16)

    def add_grams(kept):
        left = jnp.concatenate([kept[2 + kind].reshape(4 * ROWS, LANES) for kind in range(2)], axis=1)
        right = jnp.concatenate([kept[kind].reshape(4 * ROWS, LANES) for kind in range(2)], axis=1)
        full = lax.dot_general(left, right, (((0,), (0,)), ((), ())), preferred_element_type=F32)
        acc[0] += full[:LANES, :LANES]
        acc[1] += full[LANES:, LANES:]

    def body(it, _):
        unit = step * per_step + 2 * it
        for q in range(UNIT // 16):
            gather(unit + 1, x_odd, (q,))
            project(unit, 2 * it, x_even, k_even, (q,))
        add_grams(k_odd)
        after = jnp.minimum(unit + 2, units - 1)
        for q in range(UNIT // 16):
            gather(after, x_even, (q,))
            project(unit + 1, 2 * it + 1, x_odd, k_odd, (q,))
        add_grams(k_even)
        return 0

    lax.fori_loop(0, per_step // 2, body, 0)

    @pl.when(step == pl.num_programs(0) - 1)
    def _():
        add_grams(k_odd)
        stiff = 0.5 * (acc[0] + acc[0].T)
        mass = 0.5 * (acc[1] + acc[1].T)
        row, col = iota((LANES, LANES), 0), iota((LANES, LANES), 1)
        out_ref[0:LANES, :] = jnp.where(row <= col, stiff, mass)
        diag = jnp.sum(jnp.where(row == col, mass, 0.0), axis=0, keepdims=True)
        out_ref[LANES : LANES + 8, :] = jnp.broadcast_to(diag, (8, LANES))


def invert_spd(gram):
    lane = iota((8, LANES), 1)
    sub = iota((8, LANES), 0)
    regs = [gram[8 * g : 8 * g + 8, :] for g in range(16)]
    for k in range(LANES):
        own, at = k // 8, k % 8
        row = regs[own][at : at + 1, :]
        inverse = 1.0 / row[:, k : k + 1]
        row = jnp.where(lane[:1] == k, inverse, row * inverse)
        row = jnp.broadcast_to(row, (8, LANES))
        here = lane == k
        for g in range(16):
            col = jnp.broadcast_to(regs[g][:, k : k + 1], (8, LANES))
            new = jnp.where(here, 0.0, regs[g]) - col * row
            regs[g] = jnp.where(sub == at, row, new) if g == own else new
    return jnp.concatenate(regs, axis=0)


def rims(column, scale):
    elems = column.shape[0]

    def summed(rows):
        return jnp.sum(rows.T, axis=0, keepdims=True) * scale

    def side(first):
        parts = [column[pl.ds(first + c, SIDE, stride=SIDE), :] for c in range(RIM)]
        parts.append(jnp.zeros((LANES - RIM * SIDE, LANES), F32))
        return summed(jnp.concatenate(parts, axis=0))

    top = summed(column[pl.ds(0, LANES), :])
    bottom = summed(column[pl.ds(elems - LANES, LANES), :])
    left, right = side(0), side(SIDE - RIM)
    return jnp.concatenate([top, top, top, left, right, bottom, bottom, bottom], axis=0)


def rim_places(slots, count_ref, elems):
    slots = jnp.concatenate([slots, jnp.zeros((8, LANES - slots.shape[1]), jnp.int32)], axis=1)
    lane = iota((1, LANES), 1)
    row = slots // SIDE
    col = slots - row * SIDE
    k = iota(slots.shape, 0)
    across = jnp.where(k == 3, col, col - (SIDE - RIM)) * SIDE + row
    place = jnp.where(k < 3, slots, jnp.where(k < 5, across, slots - (elems - LANES)))
    live = jnp.concatenate([jnp.where(lane < count_ref[0, d], 1.0, 0.0) for d in range(8)], axis=0)
    return jnp.where(live > 0.0, place, 0), live


def energy_kernel(
    scale, gram_ref, p_hbm, dens_ref, slot_ref, count_ref, sens_ref, up_ref, down_ref, left_ref, right_ref, ritz_ref,
    p_vmem, dcol, both, total, sems
):
    elems = dcol.shape[0]
    groups = elems // GROUP
    pieces = sems.shape[0]
    span = groups // pieces
    copies = [
        pltpu.make_async_copy(
            p_hbm.at[pl.ds(i * span, span)], p_vmem.at[pl.ds(i * span, span)], sems.at[i]
        )
        for i in range(pieces)
    ]
    for copy in copies:
        copy.start()
    density_columns(dens_ref, dcol)
    slots, live = rim_places(slot_ref[...], count_ref, elems)
    tile_dens = jnp.take_along_axis(rims(dcol, 1.0 / LANES), slots, axis=1) * live

    row, col = iota((LANES, LANES), 0), iota((LANES, LANES), 1)
    packed = gram_ref[0:LANES, :]
    above = jnp.where(row < col, packed, 0.0)
    below = jnp.where(row > col, packed, 0.0)
    stiff = above + above.T + jnp.where(row == col, packed, 0.0)
    mass = below + below.T + jnp.where(row == col, gram_ref[LANES : LANES + 1, :], 0.0)
    inv_mass = invert_spd(mass)
    ritz_ref[0, 0] = jnp.sum(inv_mass * stiff) * (1.0 / LANES)
    half = jnp.dot(inv_mass, stiff, precision=HIGHEST, preferred_element_type=F32)
    sandwich = jnp.dot(half, inv_mass, precision=HIGHEST, preferred_element_type=F32)
    both[...] = jnp.zeros_like(both)
    both[0:LANES, 0:LANES] = inv_mass.astype(BF16)
    both[LANES:, LANES:] = sandwich.astype(BF16)

    per_piece = span * GROUP // UNIT
    for i in range(pieces):
        copies[i].wait()

        def body(it, _, i=i):
            unit = i * per_piece + it
            stiffs = p_vmem[pl.ds(unit * 4, 4), 0:ROWS, :].reshape(4 * ROWS, LANES)
            masses = p_vmem[pl.ds(unit * 4, 4), ROWS:, :].reshape(4 * ROWS, LANES)
            inner = jnp.dot(
                jnp.concatenate([stiffs, masses], axis=1), both[...], preferred_element_type=F32
            )
            part_stiff = (inner[:, :LANES] * stiffs.astype(F32)).reshape(4, 24, 8, LANES).sum(axis=1)
            part_mass = (inner[:, LANES:] * masses.astype(F32)).reshape(4, 24, 8, LANES).sum(axis=1)
            at = pl.ds(pl.multiple_of(unit * UNIT, UNIT), UNIT)
            dens = dcol[at, :]
            total[at, :] = 3.0 * dens * dens * part_stiff.reshape(UNIT, LANES) - part_mass.reshape(UNIT, LANES)
            return 0

        lax.fori_loop(0, per_piece, body, 0, unroll=6)

    for j in range(elems // LANES):
        block = total[pl.ds(j * LANES, LANES), :]
        sens_ref[j : j + 1, :] = jnp.sum(block.T, axis=0, keepdims=True) * scale
    tile_sens = jnp.take_along_axis(rims(total, scale), slots, axis=1) * live
    for ref, first, count in ((up_ref, 0, 3), (down_ref, 5, 3), (left_ref, 3, 1), (right_ref, 4, 1)):
        ref[...] = jnp.zeros_like(ref)
        for ch, value in enumerate((live, tile_dens, tile_sens)):
            ref[count * ch : count * ch + count, :] = value[first : first + count]


def pass_kernel(up_ref, down_ref, left_ref, right_ref, to_left_ref, to_right_ref):
    for out, own, at in ((to_left_ref, left_ref, 0), (to_right_ref, right_ref, 2)):
        out[...] = jnp.zeros_like(out)
        for ch in range(3):
            out[3 * ch : 3 * ch + 1, :] = own[ch : ch + 1, :]
            out[3 * ch + 1 : 3 * ch + 2, :] = up_ref[3 * ch + at : 3 * ch + at + 1, :]
            out[3 * ch + 2 : 3 * ch + 3, :] = down_ref[3 * ch + at : 3 * ch + at + 1, :]


def project_and_gram(connectivity, block_vectors, dens_rows, stiff_factor, mass_factor):
    elems = dens_rows.size
    groups = elems // GROUP
    steps = 9
    per_step = elems // UNIT // steps
    vmem = pl.BlockSpec(memory_space=pltpu.VMEM)
    smem = pl.BlockSpec(memory_space=pltpu.SMEM)
    return pl.pallas_call(
        lambda *refs: gram_kernel(elems, per_step, *refs),
        grid=(steps,),
        out_shape=(
            jax.ShapeDtypeStruct((groups, 2 * ROWS, LANES), BF16),
            jax.ShapeDtypeStruct((LANES + 8, LANES), F32),
        ),
        in_specs=[vmem] * 5,
        out_specs=(
            pl.BlockSpec((groups // steps, 2 * ROWS, LANES), lambda i: (i, 0, 0)),
            pl.BlockSpec((LANES + 8, LANES), lambda i: (0, 0)),
        ),
        scratch_shapes=[
            pltpu.VMEM((3 * elems + 24, LANES), F32),
            pltpu.VMEM((elems, LANES), F32),
            pltpu.VMEM((2 * ROWS, ROWS), BF16),
            pltpu.VMEM((8, elems), jnp.int32),
            pltpu.SMEM((8 * elems,), jnp.int32),
            pltpu.VMEM((UNIT // 16, ROWS, 2 * LANES), BF16),
            pltpu.VMEM((UNIT // 16, ROWS, 2 * LANES), BF16),
            pltpu.VMEM((4, UNIT // GROUP, ROWS, LANES), BF16),
            pltpu.VMEM((4, UNIT // GROUP, ROWS, LANES), BF16),
            pltpu.VMEM((2, LANES, LANES), F32),
            pltpu.SemaphoreType.DMA((8,)),
        ],
        compiler_params=pltpu.CompilerParams(vmem_limit_bytes=VMEM_LIMIT),
        name="gram",
    )(connectivity, block_vectors, dens_rows, stiff_factor, mass_factor)


def energies(scale, gram, proj, dens_rows, send_slot, send_count):
    elems = dens_rows.size
    groups = elems // GROUP
    vmem = pl.BlockSpec(memory_space=pltpu.VMEM)
    smem = pl.BlockSpec(memory_space=pltpu.SMEM)
    return pl.pallas_call(
        lambda *refs: energy_kernel(scale, *refs),
        out_shape=(
            jax.ShapeDtypeStruct((elems // LANES, LANES), F32),
            jax.ShapeDtypeStruct((16, LANES), F32),
            jax.ShapeDtypeStruct((16, LANES), F32),
            jax.ShapeDtypeStruct((8, LANES), F32),
            jax.ShapeDtypeStruct((8, LANES), F32),
            jax.ShapeDtypeStruct((1, 1), F32),
        ),
        in_specs=[vmem, pl.BlockSpec(memory_space=pl.ANY), vmem, vmem, smem],
        out_specs=(vmem,) * 5 + (smem,),
        scratch_shapes=[
            pltpu.VMEM((groups, 2 * ROWS, LANES), BF16),
            pltpu.VMEM((elems, LANES), F32),
            pltpu.VMEM((2 * LANES, 2 * LANES), BF16),
            pltpu.VMEM((elems, LANES), F32),
            pltpu.SemaphoreType.DMA((6,)),
        ],
        compiler_params=pltpu.CompilerParams(vmem_limit_bytes=VMEM_LIMIT),
        name="energy",
    )(gram, proj, dens_rows, send_slot, send_count)


def split3(value):
    high = value.astype(BF16)
    rest = value - high.astype(F32)
    mid = rest.astype(BF16)
    low = (rest - mid.astype(F32)).astype(BF16)
    return high, mid, low


def owner_kernel(up_ref, down_ref, left_ref, right_ref, target_ref, weight_ref, dens_ref, sens_ref, fdens_ref, fsens_ref):
    lane = iota((1, LANES), 1)

    def lanes_of(main, corner):
        return jnp.where(lane < 96, main, pltpu.roll(corner, 96, 1))

    def by_side(table):
        table = jnp.concatenate([table, jnp.zeros((8, LANES - table.shape[1]), table.dtype)], axis=1)
        pairs = ((1, 0), (6, 5), (3, 2), (4, 7))
        return [lanes_of(table[m : m + 1], table[c : c + 1]) for m, c in pairs]

    weights = by_side(weight_ref[...])
    targets = jnp.concatenate(by_side(target_ref[...]), axis=1)
    values = [[], [], []]
    for ch in range(3):
        up = up_ref[3 * ch + 1 : 3 * ch + 2, :]
        down = down_ref[3 * ch + 1 : 3 * ch + 2, :]
        left = left_ref[3 * ch : 3 * ch + 3, :]
        right = right_ref[3 * ch : 3 * ch + 3, :]
        sides = (
            lanes_of(up, left[1:2]),
            lanes_of(down, left[2:3]),
            lanes_of(left[0:1], right[1:2]),
            lanes_of(right[0:1], right[2:3]),
        )
        for side in range(4):
            values[ch].append(sides[side] * weights[side])
    stacked = jnp.concatenate([jnp.concatenate(v, axis=1) for v in values], axis=0)
    high, mid, low = split3(stacked)
    left = jnp.concatenate([high, mid, low, jnp.zeros((7, 4 * LANES), BF16)], axis=0)
    for j in range(dens_ref.shape[0]):
        hit = targets == iota((LANES, 4 * LANES), 0) + j * LANES
        hot = jnp.where(hit, 1.0, 0.0).astype(BF16)
        sums = lax.dot_general(left, hot, (((1,), (1,)), ((), ())), preferred_element_type=F32)
        sums = sums[0:3] + sums[3:6] + sums[6:9]
        under = 1.0 + sums[0:1]
        fdens_ref[j : j + 1, :] = (dens_ref[j : j + 1, :] + sums[1:2]) / under
        fsens_ref[j : j + 1, :] = (sens_ref[j : j + 1, :] + sums[2:3]) / under


def place(index, sizes):
    rows, cols = sizes
    return [index // cols // 2, index // cols % 2, index % cols // 4, index % 4]


def swapped(sizes, axis, step):
    rows, cols = sizes
    lengths = [rows // 2, 2, cols // 4, 4]
    pairs = []
    for i in range(rows * cols):
        at = place(i, sizes)
        at[axis] = (at[axis] + step) % lengths[axis]
        pairs.append((i, ((at[0] * 2 + at[1]) * lengths[2] + at[2]) * 4 + at[3]))
    return pairs


def sum_over_devices(value, sizes):
    value = value + lax.ppermute(value, AXES, swapped(sizes, 1, 1))
    lengths = [sizes[0] // 2, 2, sizes[1] // 4, 4]
    for axis in (3, 2, 0):
        others = [lax.ppermute(value, AXES, swapped(sizes, axis, s)) for s in range(1, lengths[axis])]
        for other in others:
            value = value + other
    return value


def torus(axis, step):
    size = lax.axis_size(axis)
    return [(i, (i + step) % size) for i in range(size)]


def per_device(
    block_vectors, connectivity, density, stiff_factor, mass_factor, send_slot, send_count, recv_target, recv_weight
):
    vec_count = block_vectors.shape[1]
    elems = density.shape[0]
    sizes = (lax.axis_size("gx"), lax.axis_size("gy"))
    scale = float(elems * sizes[0] * sizes[1]) / vec_count

    dens_rows = density.reshape(elems // LANES, LANES)

    proj, gram = project_and_gram(connectivity, block_vectors, dens_rows, stiff_factor, mass_factor)
    gram = sum_over_devices(gram, sizes)

    sens_rows, up, down, left, right, ritz = energies(scale, gram, proj, dens_rows, send_slot[0], send_count)

    up = lax.ppermute(up, "gx", torus("gx", -1))
    down = lax.ppermute(down, "gx", torus("gx", 1))
    vmem = pl.BlockSpec(memory_space=pltpu.VMEM)
    left, right = pl.pallas_call(
        pass_kernel,
        out_shape=(jax.ShapeDtypeStruct((16, LANES), F32),) * 2,
        in_specs=[vmem] * 4,
        out_specs=(vmem, vmem),
        name="pass_on",
    )(up, down, left, right)
    left = lax.ppermute(left, "gy", torus("gy", -1))
    right = lax.ppermute(right, "gy", torus("gy", 1))

    fdens, fsens = pl.pallas_call(
        owner_kernel,
        out_shape=(jax.ShapeDtypeStruct((elems // LANES, LANES), F32),) * 2,
        in_specs=[vmem] * 8,
        out_specs=(vmem, vmem),
        name="owner",
    )(up, down, left, right, recv_target[0], recv_weight[0], dens_rows, sens_rows)
    return fdens.reshape(elems), fsens.reshape(elems), ritz.reshape(())


def solution(mesh):
    placed = (
        P(None, None, ("gx", "gy")),
        P(None, ("gx", "gy")),
        P(("gx", "gy")),
        P(),
        P(),
        P(("gx", "gy"), None, None),
        P(("gx", "gy"), None),
        P(("gx", "gy"), None, None),
        P(("gx", "gy"), None, None),
    )
    return jax.shard_map(
        per_device,
        mesh=mesh,
        in_specs=placed,
        out_specs=(P(("gx", "gy")), P(("gx", "gy")), P()),
        check_vma=False,
    )
```

```python
import jax
import jax.numpy as jnp
from jax import lax
from jax.experimental import pallas as pl
from jax.experimental.pallas import tpu as pltpu
from jax.sharding import PartitionSpec as P

SIDE = 48
RIM = 2
LANES = 128
GROUP = 8
UNIT = 128
STRIP = 32
ROWS = 24 * GROUP
AXES = ("gx", "gy")
VMEM_LIMIT = 60 * 1024 * 1024
F32 = jnp.float32
BF16 = jnp.bfloat16
HIGHEST = lax.Precision.HIGHEST


def iota(shape, dim):
    return lax.broadcasted_iota(jnp.int32, shape, dim)


def density_columns(dens_ref, dcol):
    for j in range(dens_ref.shape[0]):
        row = jnp.broadcast_to(dens_ref[j : j + 1, :], (LANES, LANES))
        dcol[pl.ds(j * LANES, LANES), :] = row.T


PIECES = (
    ((0, 0), (1, 3), (2, 6)),
    ((2, -2), (3, 1), (4, 4), (5, 7)),
    ((5, -1), (6, 2), (7, 5)),
)


def spread(factor):
    dofs = factor.shape[0]
    wide, tall = (ROWS, dofs), (dofs, ROWS)
    take_row = (iota(wide, 0) >> 3) == iota(wide, 1)
    out = iota(tall, 1)
    within = lax.rem(out, dofs)
    corner = within // 3
    take_col = (within - 3 * corner) * 8 + corner == iota(tall, 0)
    picked = jnp.dot(jnp.where(take_row, 1.0, 0.0).astype(BF16), factor, preferred_element_type=F32)
    full = jnp.dot(picked.astype(BF16), jnp.where(take_col, 1.0, 0.0).astype(BF16), preferred_element_type=F32)
    square = (ROWS, ROWS)
    same = (iota(square, 0) & 7) == iota(square, 1) // dofs
    return jnp.where(same, full, 0.0).astype(BF16)


def gram_kernel(
    elems, per_step, conn_ref, vec_ref, dens_ref, stiff_ref, mass_ref, p_ref, out_ref,
    table, dcol, w_ref, tripled, rows_smem, x_even, x_odd, k_even, k_odd, acc, sem
):
    step = pl.program_id(0)
    units = elems // UNIT
    sub = iota((8, LANES), 0)

    def gather(unit, xbuf, qs=tuple(range(UNIT // 16))):
        base = unit * UNIT
        for q in qs:
            for h in range(2):
                for pair in range(4):
                    regs = []
                    for e in range(2):
                        at = base + (q * 16 + h * 8 + pair * 2 + e)
                        rows = [rows_smem[a * elems + at] for a in range(8)]
                        for pieces in PIECES:
                            value = None
                            for corner, first in pieces:
                                got = table[pl.ds(rows[corner] + (8 - first), 8), :]
                                value = got if value is None else jnp.where(sub >= first, got, value)
                            regs.append(value)
                    block = jnp.concatenate(regs, axis=0).astype(BF16)
                    xbuf[q, pl.ds(pair * 48, 48), pl.ds(h * LANES, LANES)] = block

    @pl.when(step == 0)
    def _():
        tripled[...] = conn_ref[...] * 3
        copies = [
            pltpu.make_async_copy(tripled.at[a], rows_smem.at[pl.ds(a * elems, elems)], sem.at[a]) for a in range(8)
        ]
        for copy in copies:
            copy.start()
        w_ref[0:ROWS] = spread(stiff_ref[...])
        w_ref[ROWS:] = spread(mass_ref[...])
        for c in range(3):
            for j in range(elems // LANES):
                block = vec_ref[c, :, pl.ds(j * LANES, LANES)].astype(F32).T
                table[pl.ds(8 + 3 * LANES * j + c, LANES, stride=3), :] = block
        density_columns(dens_ref, dcol)
        acc[...] = jnp.zeros_like(acc)
        k_odd[...] = jnp.zeros_like(k_odd)
        for copy in copies:
            copy.wait()
        gather(0, x_even)

    def project(unit, local, xbuf, kept, qs):
        for q in qs:
            full = jnp.dot(w_ref[...], xbuf[q], preferred_element_type=F32).astype(BF16)
            for h in range(2):
                part = full[:, h * LANES : (h + 1) * LANES]
                chunk = 2 * q + h
                p_ref[local * (UNIT // GROUP) + chunk] = part
                wide = part.astype(F32).reshape(2, 24, 8, LANES)
                dens = dcol[pl.ds(pl.multiple_of(unit * UNIT + chunk * 8, 8), 8), :]
                for kind, factor in enumerate((dens * dens * dens, dens)):
                    kept[kind, chunk] = part[kind * ROWS : (kind + 1) * ROWS]
                    kept[2 + kind, chunk] = (wide[kind] * factor[None]).reshape(ROWS, LANES).astype(BF16)

    def add_grams(kept):
        left = jnp.concatenate([kept[2 + kind].reshape(UNIT // GROUP * ROWS, LANES) for kind in range(2)], axis=1)
        right = jnp.concatenate([kept[kind].reshape(UNIT // GROUP * ROWS, LANES) for kind in range(2)], axis=1)
        full = lax.dot_general(left, right, (((0,), (0,)), ((), ())), preferred_element_type=F32)
        acc[0] += full[:LANES, :LANES]
        acc[1] += full[LANES:, LANES:]

    def body(it, _):
        unit = step * per_step + 2 * it
        for q in range(UNIT // 16):
            gather(unit + 1, x_odd, (q,))
            project(unit, 2 * it, x_even, k_even, (q,))
        add_grams(k_odd)
        after = jnp.minimum(unit + 2, units - 1)
        for q in range(UNIT // 16):
            gather(after, x_even, (q,))
            project(unit + 1, 2 * it + 1, x_odd, k_odd, (q,))
        add_grams(k_even)
        return 0

    lax.fori_loop(0, per_step // 2, body, 0)

    @pl.when(step == pl.num_programs(0) - 1)
    def _():
        add_grams(k_odd)
        stiff = 0.5 * (acc[0] + acc[0].T)
        mass = 0.5 * (acc[1] + acc[1].T)
        row, col = iota((LANES, LANES), 0), iota((LANES, LANES), 1)
        out_ref[0:LANES, :] = jnp.where(row <= col, stiff, mass)
        diag = jnp.sum(jnp.where(row == col, mass, 0.0), axis=0, keepdims=True)
        out_ref[LANES : LANES + 8, :] = jnp.broadcast_to(diag, (8, LANES))


def invert_spd(gram):
    lane = iota((8, LANES), 1)
    sub = iota((8, LANES), 0)

    def column(reg, k):
        return jnp.broadcast_to(reg[:, k : k + 1], (8, LANES))

    def row(reg, k):
        return jnp.broadcast_to(reg[k : k + 1, :], (8, LANES))

    regs = [gram[8 * g : 8 * g + 8, :] for g in range(LANES // 8)]
    for own in range(LANES // 8):
        first = 8 * own
        inside = (lane >= first) & (lane < first + 8)
        cols = [[column(reg, first + j) for j in range(8)] for reg in regs]
        held = list(cols[own])
        panel = jnp.where(inside, jnp.where(lane == first + sub, 1.0, 0.0), regs[own])
        for k in range(8):
            inverse = 1.0 / row(held[k], k)
            here = sub == k
            for at in range(k + 1, 9):
                value = held[at] if at < 8 else panel
                pivot = row(value, k)
                value = jnp.where(here, 0.0, value) - jnp.where(here, -pivot, held[k] * pivot) * inverse
                if at < 8:
                    held[at] = value
                else:
                    panel = value
        rows = [row(panel, j) for j in range(8)]
        for g in range(LANES // 8):
            if g == own:
                regs[g] = panel
                continue
            value = jnp.where(inside, 0.0, regs[g])
            for j in range(8):
                value = value - cols[g][j] * rows[j]
            regs[g] = value
    return jnp.concatenate(regs, axis=0)


def rims(column, scale):
    elems = column.shape[0]

    def summed(rows):
        return jnp.sum(rows.T, axis=0, keepdims=True) * scale

    def side(first):
        parts = [column[pl.ds(first + c, SIDE, stride=SIDE), :] for c in range(RIM)]
        parts.append(jnp.zeros((LANES - RIM * SIDE, LANES), F32))
        return summed(jnp.concatenate(parts, axis=0))

    top = summed(column[pl.ds(0, LANES), :])
    bottom = summed(column[pl.ds(elems - LANES, LANES), :])
    left, right = side(0), side(SIDE - RIM)
    return jnp.concatenate([top, top, top, left, right, bottom, bottom, bottom], axis=0)


def rim_places(slots, count_ref, elems):
    slots = jnp.concatenate([slots, jnp.zeros((8, LANES - slots.shape[1]), jnp.int32)], axis=1)
    lane = iota((1, LANES), 1)
    row = slots // SIDE
    col = slots - row * SIDE
    k = iota(slots.shape, 0)
    across = jnp.where(k == 3, col, col - (SIDE - RIM)) * SIDE + row
    place = jnp.where(k < 3, slots, jnp.where(k < 5, across, slots - (elems - LANES)))
    live = jnp.concatenate([jnp.where(lane < count_ref[0, d], 1.0, 0.0) for d in range(8)], axis=0)
    return jnp.where(live > 0.0, place, 0), live


def energy_kernel(
    scale, gram_ref, p_hbm, dens_ref, slot_ref, count_ref, sens_ref, up_ref, down_ref, left_ref, right_ref, ritz_ref,
    p_vmem, dcol, both, total, sems
):
    elems = dcol.shape[0]
    groups = elems // GROUP
    pieces = sems.shape[0]
    span = groups // pieces
    copies = [
        pltpu.make_async_copy(
            p_hbm.at[pl.ds(i * span, span)], p_vmem.at[pl.ds(i * span, span)], sems.at[i]
        )
        for i in range(pieces)
    ]
    for copy in copies:
        copy.start()
    density_columns(dens_ref, dcol)
    slots, live = rim_places(slot_ref[...], count_ref, elems)
    tile_dens = jnp.take_along_axis(rims(dcol, 1.0 / LANES), slots, axis=1) * live

    row, col = iota((LANES, LANES), 0), iota((LANES, LANES), 1)
    packed = gram_ref[0:LANES, :]
    above = jnp.where(row < col, packed, 0.0)
    below = jnp.where(row > col, packed, 0.0)
    stiff = above + above.T + jnp.where(row == col, packed, 0.0)
    mass = below + below.T + jnp.where(row == col, gram_ref[LANES : LANES + 1, :], 0.0)
    inv_mass = invert_spd(mass)
    ritz_ref[0, 0] = jnp.sum(inv_mass * stiff) * (1.0 / LANES)
    half = jnp.dot(inv_mass, stiff, precision=HIGHEST, preferred_element_type=F32)
    sandwich = jnp.dot(half, inv_mass, precision=HIGHEST, preferred_element_type=F32)
    both[...] = jnp.zeros_like(both)
    both[0:LANES, 0:LANES] = inv_mass.astype(BF16)
    both[LANES:, LANES:] = sandwich.astype(BF16)

    per_piece = span * GROUP // STRIP
    for i in range(pieces):
        copies[i].wait()

        def body(it, _, i=i):
            unit = i * per_piece + it
            stiffs = p_vmem[pl.ds(unit * (STRIP // GROUP), STRIP // GROUP), 0:ROWS, :].reshape(STRIP // GROUP * ROWS, LANES)
            masses = p_vmem[pl.ds(unit * (STRIP // GROUP), STRIP // GROUP), ROWS:, :].reshape(STRIP // GROUP * ROWS, LANES)
            inner = jnp.dot(
                jnp.concatenate([stiffs, masses], axis=1), both[...], preferred_element_type=F32
            )
            part_stiff = (inner[:, :LANES] * stiffs.astype(F32)).reshape(STRIP // GROUP, 24, 8, LANES).sum(axis=1)
            part_mass = (inner[:, LANES:] * masses.astype(F32)).reshape(STRIP // GROUP, 24, 8, LANES).sum(axis=1)
            at = pl.ds(pl.multiple_of(unit * STRIP, STRIP), STRIP)
            dens = dcol[at, :]
            total[at, :] = 3.0 * dens * dens * part_stiff.reshape(STRIP, LANES) - part_mass.reshape(STRIP, LANES)
            return 0

        lax.fori_loop(0, per_piece, body, 0, unroll=12)

    for j in range(elems // LANES):
        block = total[pl.ds(j * LANES, LANES), :]
        sens_ref[j : j + 1, :] = jnp.sum(block.T, axis=0, keepdims=True) * scale
    tile_sens = jnp.take_along_axis(rims(total, scale), slots, axis=1) * live
    for ref, first, count in ((up_ref, 0, 3), (down_ref, 5, 3), (left_ref, 3, 1), (right_ref, 4, 1)):
        ref[...] = jnp.zeros_like(ref)
        for ch, value in enumerate((live, tile_dens, tile_sens)):
            ref[count * ch : count * ch + count, :] = value[first : first + count]


def pass_kernel(up_ref, down_ref, left_ref, right_ref, to_left_ref, to_right_ref):
    for out, own, at in ((to_left_ref, left_ref, 0), (to_right_ref, right_ref, 2)):
        out[...] = jnp.zeros_like(out)
        for ch in range(3):
            out[3 * ch : 3 * ch + 1, :] = own[ch : ch + 1, :]
            out[3 * ch + 1 : 3 * ch + 2, :] = up_ref[3 * ch + at : 3 * ch + at + 1, :]
            out[3 * ch + 2 : 3 * ch + 3, :] = down_ref[3 * ch + at : 3 * ch + at + 1, :]


def project_and_gram(connectivity, block_vectors, dens_rows, stiff_factor, mass_factor):
    elems = dens_rows.size
    groups = elems // GROUP
    steps = 9
    per_step = elems // UNIT // steps
    vmem = pl.BlockSpec(memory_space=pltpu.VMEM)
    smem = pl.BlockSpec(memory_space=pltpu.SMEM)
    return pl.pallas_call(
        lambda *refs: gram_kernel(elems, per_step, *refs),
        grid=(steps,),
        out_shape=(
            jax.ShapeDtypeStruct((groups, 2 * ROWS, LANES), BF16),
            jax.ShapeDtypeStruct((LANES + 8, LANES), F32),
        ),
        in_specs=[vmem] * 5,
        out_specs=(
            pl.BlockSpec((groups // steps, 2 * ROWS, LANES), lambda i: (i, 0, 0)),
            pl.BlockSpec((LANES + 8, LANES), lambda i: (0, 0)),
        ),
        scratch_shapes=[
            pltpu.VMEM((3 * elems + 24, LANES), F32),
            pltpu.VMEM((elems, LANES), F32),
            pltpu.VMEM((2 * ROWS, ROWS), BF16),
            pltpu.VMEM((8, elems), jnp.int32),
            pltpu.SMEM((8 * elems,), jnp.int32),
            pltpu.VMEM((UNIT // 16, ROWS, 2 * LANES), BF16),
            pltpu.VMEM((UNIT // 16, ROWS, 2 * LANES), BF16),
            pltpu.VMEM((4, UNIT // GROUP, ROWS, LANES), BF16),
            pltpu.VMEM((4, UNIT // GROUP, ROWS, LANES), BF16),
            pltpu.VMEM((2, LANES, LANES), F32),
            pltpu.SemaphoreType.DMA((8,)),
        ],
        compiler_params=pltpu.CompilerParams(vmem_limit_bytes=VMEM_LIMIT),
        name="gram",
    )(connectivity, block_vectors, dens_rows, stiff_factor, mass_factor)


def energies(scale, gram, proj, dens_rows, send_slot, send_count):
    elems = dens_rows.size
    groups = elems // GROUP
    vmem = pl.BlockSpec(memory_space=pltpu.VMEM)
    smem = pl.BlockSpec(memory_space=pltpu.SMEM)
    return pl.pallas_call(
        lambda *refs: energy_kernel(scale, *refs),
        out_shape=(
            jax.ShapeDtypeStruct((elems // LANES, LANES), F32),
            jax.ShapeDtypeStruct((16, LANES), F32),
            jax.ShapeDtypeStruct((16, LANES), F32),
            jax.ShapeDtypeStruct((8, LANES), F32),
            jax.ShapeDtypeStruct((8, LANES), F32),
            jax.ShapeDtypeStruct((1, 1), F32),
        ),
        in_specs=[vmem, pl.BlockSpec(memory_space=pl.ANY), vmem, vmem, smem],
        out_specs=(vmem,) * 5 + (smem,),
        scratch_shapes=[
            pltpu.VMEM((groups, 2 * ROWS, LANES), BF16),
            pltpu.VMEM((elems, LANES), F32),
            pltpu.VMEM((2 * LANES, 2 * LANES), BF16),
            pltpu.VMEM((elems, LANES), F32),
            pltpu.SemaphoreType.DMA((6,)),
        ],
        compiler_params=pltpu.CompilerParams(vmem_limit_bytes=VMEM_LIMIT),
        name="energy",
    )(gram, proj, dens_rows, send_slot, send_count)


def split3(value):
    high = value.astype(BF16)
    rest = value - high.astype(F32)
    mid = rest.astype(BF16)
    low = (rest - mid.astype(F32)).astype(BF16)
    return high, mid, low


def owner_kernel(up_ref, down_ref, left_ref, right_ref, target_ref, weight_ref, dens_ref, sens_ref, fdens_ref, fsens_ref):
    lane = iota((1, LANES), 1)

    def lanes_of(main, corner):
        return jnp.where(lane < 96, main, pltpu.roll(corner, 96, 1))

    def by_side(table):
        table = jnp.concatenate([table, jnp.zeros((8, LANES - table.shape[1]), table.dtype)], axis=1)
        pairs = ((1, 0), (6, 5), (3, 2), (4, 7))
        return [lanes_of(table[m : m + 1], table[c : c + 1]) for m, c in pairs]

    weights = by_side(weight_ref[...])
    targets = jnp.concatenate(by_side(target_ref[...]), axis=1)
    values = [[], [], []]
    for ch in range(3):
        up = up_ref[3 * ch + 1 : 3 * ch + 2, :]
        down = down_ref[3 * ch + 1 : 3 * ch + 2, :]
        left = left_ref[3 * ch : 3 * ch + 3, :]
        right = right_ref[3 * ch : 3 * ch + 3, :]
        sides = (
            lanes_of(up, left[1:2]),
            lanes_of(down, left[2:3]),
            lanes_of(left[0:1], right[1:2]),
            lanes_of(right[0:1], right[2:3]),
        )
        for side in range(4):
            values[ch].append(sides[side] * weights[side])
    stacked = jnp.concatenate([jnp.concatenate(v, axis=1) for v in values], axis=0)
    high, mid, low = split3(stacked)
    left = jnp.concatenate([high, mid, low, jnp.zeros((7, 4 * LANES), BF16)], axis=0)
    last = dens_ref.shape[0] - 1
    for j in range(last + 1):
        part = slice(0 if j in (0, last) else 2 * LANES, 4 * LANES)
        hit = targets[:, part] == iota((LANES, part.stop - part.start), 0) + j * LANES
        hot = jnp.where(hit, 1.0, 0.0).astype(BF16)
        sums = lax.dot_general(left[:, part], hot, (((1,), (1,)), ((), ())), preferred_element_type=F32)
        sums = sums[0:3] + sums[3:6] + sums[6:9]
        under = 1.0 + sums[0:1]
        fdens_ref[j : j + 1, :] = (dens_ref[j : j + 1, :] + sums[1:2]) / under
        fsens_ref[j : j + 1, :] = (sens_ref[j : j + 1, :] + sums[2:3]) / under


def place(index, sizes):
    rows, cols = sizes
    return [index // cols // 2, index // cols % 2, index % cols // 4, index % 4]


def swapped(sizes, axis, step):
    rows, cols = sizes
    lengths = [rows // 2, 2, cols // 4, 4]
    pairs = []
    for i in range(rows * cols):
        at = place(i, sizes)
        at[axis] = (at[axis] + step) % lengths[axis]
        pairs.append((i, ((at[0] * 2 + at[1]) * lengths[2] + at[2]) * 4 + at[3]))
    return pairs


def sum_over_devices(value, sizes):
    value = value + lax.ppermute(value, AXES, swapped(sizes, 1, 1))
    lengths = [sizes[0] // 2, 2, sizes[1] // 4, 4]
    for axis in (3, 2, 0):
        others = [lax.ppermute(value, AXES, swapped(sizes, axis, s)) for s in range(1, lengths[axis])]
        for other in others:
            value = value + other
    return value


def torus(axis, step):
    size = lax.axis_size(axis)
    return [(i, (i + step) % size) for i in range(size)]


def per_device(
    block_vectors, connectivity, density, stiff_factor, mass_factor, send_slot, send_count, recv_target, recv_weight
):
    vec_count = block_vectors.shape[1]
    elems = density.shape[0]
    sizes = (lax.axis_size("gx"), lax.axis_size("gy"))
    scale = float(elems * sizes[0] * sizes[1]) / vec_count

    dens_rows = density.reshape(elems // LANES, LANES)

    proj, gram = project_and_gram(connectivity, block_vectors, dens_rows, stiff_factor, mass_factor)
    gram = sum_over_devices(gram, sizes)

    sens_rows, up, down, left, right, ritz = energies(scale, gram, proj, dens_rows, send_slot[0], send_count)

    up = lax.ppermute(up, "gx", torus("gx", -1))
    down = lax.ppermute(down, "gx", torus("gx", 1))
    vmem = pl.BlockSpec(memory_space=pltpu.VMEM)
    left, right = pl.pallas_call(
        pass_kernel,
        out_shape=(jax.ShapeDtypeStruct((16, LANES), F32),) * 2,
        in_specs=[vmem] * 4,
        out_specs=(vmem, vmem),
        name="pass_on",
    )(up, down, left, right)
    left = lax.ppermute(left, "gy", torus("gy", -1))
    right = lax.ppermute(right, "gy", torus("gy", 1))

    fdens, fsens = pl.pallas_call(
        owner_kernel,
        out_shape=(jax.ShapeDtypeStruct((elems // LANES, LANES), F32),) * 2,
        in_specs=[vmem] * 8,
        out_specs=(vmem, vmem),
        name="owner",
    )(up, down, left, right, recv_target[0], recv_weight[0], dens_rows, sens_rows)
    return fdens.reshape(elems), fsens.reshape(elems), ritz.reshape(())


def solution(mesh):
    placed = (
        P(None, None, ("gx", "gy")),
        P(None, ("gx", "gy")),
        P(("gx", "gy")),
        P(),
        P(),
        P(("gx", "gy"), None, None),
        P(("gx", "gy"), None),
        P(("gx", "gy"), None, None),
        P(("gx", "gy"), None, None),
    )
    return jax.shard_map(
        per_device,
        mesh=mesh,
        in_specs=placed,
        out_specs=(P(("gx", "gy")), P(("gx", "gy")), P()),
        check_vma=False,
    )
```

```python
import jax
import jax.numpy as jnp
from jax import lax
from jax.experimental import pallas as pl
from jax.experimental.pallas import tpu as pltpu
from jax.sharding import PartitionSpec as P

SIDE = 48
RIM = 2
LANES = 128
GROUP = 8
UNIT = 128
STRIP = 32
ROWS = 24 * GROUP
AXES = ("gx", "gy")
VMEM_LIMIT = 44 * 1024 * 1024
F32 = jnp.float32
BF16 = jnp.bfloat16
HIGHEST = lax.Precision.HIGHEST


def iota(shape, dim):
    return lax.broadcasted_iota(jnp.int32, shape, dim)


def density_columns(dens_ref, dcol):
    for j in range(dens_ref.shape[0]):
        row = jnp.broadcast_to(dens_ref[j : j + 1, :], (LANES, LANES))
        dcol[pl.ds(j * LANES, LANES), :] = row.T


PIECES = (
    ((0, 0), (1, 3), (2, 6)),
    ((2, -2), (3, 1), (4, 4), (5, 7)),
    ((5, -1), (6, 2), (7, 5)),
)


def spread(factor):
    dofs = factor.shape[0]
    wide, tall = (ROWS, dofs), (dofs, ROWS)
    take_row = (iota(wide, 0) >> 3) == iota(wide, 1)
    out = iota(tall, 1)
    within = lax.rem(out, dofs)
    corner = within // 3
    take_col = (within - 3 * corner) * 8 + corner == iota(tall, 0)
    picked = jnp.dot(jnp.where(take_row, 1.0, 0.0).astype(BF16), factor, preferred_element_type=F32)
    full = jnp.dot(picked.astype(BF16), jnp.where(take_col, 1.0, 0.0).astype(BF16), preferred_element_type=F32)
    square = (ROWS, ROWS)
    same = (iota(square, 0) & 7) == iota(square, 1) // dofs
    return jnp.where(same, full, 0.0).astype(BF16)


def gram_kernel(
    elems, per_step, conn_ref, vec_ref, dens_ref, stiff_ref, mass_ref, p_ref, out_ref,
    table, dcol, w_ref, tripled, rows_smem, x_even, x_odd, k_even, k_odd, acc, sem
):
    step = pl.program_id(0)
    units = elems // UNIT
    sub = iota((8, LANES), 0)

    def gather(unit, xbuf, qs=tuple(range(UNIT // 16))):
        base = unit * UNIT
        for q in qs:
            for h in range(2):
                for pair in range(4):
                    regs = []
                    for e in range(2):
                        at = base + (q * 16 + h * 8 + pair * 2 + e)
                        rows = [rows_smem[a * elems + at] for a in range(8)]
                        for pieces in PIECES:
                            value = None
                            for corner, first in pieces:
                                got = table[pl.ds(rows[corner] + (8 - first), 8), :]
                                value = got if value is None else jnp.where(sub >= first, got, value)
                            regs.append(value)
                    block = jnp.concatenate(regs, axis=0).astype(BF16)
                    xbuf[q, pl.ds(pair * 48, 48), pl.ds(h * LANES, LANES)] = block

    @pl.when(step == 0)
    def _():
        tripled[...] = conn_ref[...] * 3
        copies = [
            pltpu.make_async_copy(tripled.at[a], rows_smem.at[pl.ds(a * elems, elems)], sem.at[a]) for a in range(8)
        ]
        for copy in copies:
            copy.start()
        w_ref[0:ROWS] = spread(stiff_ref[...])
        w_ref[ROWS:] = spread(mass_ref[...])
        for c in range(3):
            for j in range(elems // LANES):
                block = vec_ref[c, :, pl.ds(j * LANES, LANES)].astype(F32).T
                table[pl.ds(8 + 3 * LANES * j + c, LANES, stride=3), :] = block
        density_columns(dens_ref, dcol)
        acc[...] = jnp.zeros_like(acc)
        k_odd[...] = jnp.zeros_like(k_odd)
        for copy in copies:
            copy.wait()
        gather(0, x_even)

    def project(unit, local, xbuf, kept, qs):
        for q in qs:
            full = jnp.dot(w_ref[...], xbuf[q], preferred_element_type=F32).astype(BF16)
            for h in range(2):
                part = full[:, h * LANES : (h + 1) * LANES]
                chunk = 2 * q + h
                p_ref[local * (UNIT // GROUP) + chunk] = part
                wide = part.astype(F32).reshape(2, 24, 8, LANES)
                dens = dcol[pl.ds(pl.multiple_of(unit * UNIT + chunk * 8, 8), 8), :]
                for kind, factor in enumerate((dens * dens * dens, dens)):
                    kept[kind, chunk] = part[kind * ROWS : (kind + 1) * ROWS]
                    kept[2 + kind, chunk] = (wide[kind] * factor[None]).reshape(ROWS, LANES).astype(BF16)

    def add_grams(kept):
        left = jnp.concatenate([kept[2 + kind].reshape(UNIT // GROUP * ROWS, LANES) for kind in range(2)], axis=1)
        right = jnp.concatenate([kept[kind].reshape(UNIT // GROUP * ROWS, LANES) for kind in range(2)], axis=1)
        full = lax.dot_general(left, right, (((0,), (0,)), ((), ())), preferred_element_type=F32)
        acc[0] += full[:LANES, :LANES]
        acc[1] += full[LANES:, LANES:]

    def body(it, _):
        unit = step * per_step + 2 * it
        for q in range(UNIT // 16):
            gather(unit + 1, x_odd, (q,))
            project(unit, 2 * it, x_even, k_even, (q,))
        add_grams(k_odd)
        after = jnp.minimum(unit + 2, units - 1)
        for q in range(UNIT // 16):
            gather(after, x_even, (q,))
            project(unit + 1, 2 * it + 1, x_odd, k_odd, (q,))
        add_grams(k_even)
        return 0

    lax.fori_loop(0, per_step // 2, body, 0)

    @pl.when(step == pl.num_programs(0) - 1)
    def _():
        add_grams(k_odd)
        stiff = 0.5 * (acc[0] + acc[0].T)
        mass = 0.5 * (acc[1] + acc[1].T)
        row, col = iota((LANES, LANES), 0), iota((LANES, LANES), 1)
        out_ref[0:LANES, :] = jnp.where(row <= col, stiff, mass)
        diag = jnp.sum(jnp.where(row == col, mass, 0.0), axis=0, keepdims=True)
        out_ref[LANES : LANES + 8, :] = jnp.broadcast_to(diag, (8, LANES))


def invert_spd(gram):
    lane = iota((8, LANES), 1)
    sub = iota((8, LANES), 0)

    def column(reg, k):
        return jnp.broadcast_to(reg[:, k : k + 1], (8, LANES))

    def row(reg, k):
        return jnp.broadcast_to(reg[k : k + 1, :], (8, LANES))

    regs = [gram[8 * g : 8 * g + 8, :] for g in range(LANES // 8)]
    for own in range(LANES // 8):
        first = 8 * own
        inside = (lane >= first) & (lane < first + 8)
        cols = [[column(reg, first + j) for j in range(8)] for reg in regs]
        held = list(cols[own])
        panel = jnp.where(inside, jnp.where(lane == first + sub, 1.0, 0.0), regs[own])
        for k in range(8):
            inverse = 1.0 / row(held[k], k)
            here = sub == k
            for at in range(k + 1, 9):
                value = held[at] if at < 8 else panel
                pivot = row(value, k)
                value = jnp.where(here, 0.0, value) - jnp.where(here, -pivot, held[k] * pivot) * inverse
                if at < 8:
                    held[at] = value
                else:
                    panel = value
        rows = [row(panel, j) for j in range(8)]
        for g in range(LANES // 8):
            if g == own:
                regs[g] = panel
                continue
            value = jnp.where(inside, 0.0, regs[g])
            for j in range(8):
                value = value - cols[g][j] * rows[j]
            regs[g] = value
    return jnp.concatenate(regs, axis=0)


def rims(column, scale):
    elems = column.shape[0]

    def summed(rows):
        return jnp.sum(rows.T, axis=0, keepdims=True) * scale

    def side(first):
        parts = [column[pl.ds(first + c, SIDE, stride=SIDE), :] for c in range(RIM)]
        parts.append(jnp.zeros((LANES - RIM * SIDE, LANES), F32))
        return summed(jnp.concatenate(parts, axis=0))

    top = summed(column[pl.ds(0, LANES), :])
    bottom = summed(column[pl.ds(elems - LANES, LANES), :])
    left, right = side(0), side(SIDE - RIM)
    return jnp.concatenate([top, top, top, left, right, bottom, bottom, bottom], axis=0)


def rim_places(slots, count_ref, elems):
    slots = jnp.concatenate([slots, jnp.zeros((8, LANES - slots.shape[1]), jnp.int32)], axis=1)
    lane = iota((1, LANES), 1)
    row = slots // SIDE
    col = slots - row * SIDE
    k = iota(slots.shape, 0)
    across = jnp.where(k == 3, col, col - (SIDE - RIM)) * SIDE + row
    place = jnp.where(k < 3, slots, jnp.where(k < 5, across, slots - (elems - LANES)))
    live = jnp.concatenate([jnp.where(lane < count_ref[0, d], 1.0, 0.0) for d in range(8)], axis=0)
    return jnp.where(live > 0.0, place, 0), live


def energy_kernel(
    scale, gram_any, p_hbm, dens_ref, slot_ref, count_ref, sens_ref, up_ref, down_ref, side_ref, ritz_ref,
    gram_ref, p_vmem, dcol, both, total, gram_sem, sems
):
    elems = dcol.shape[0]
    groups = elems // GROUP
    pieces = sems.shape[0]
    span = groups // pieces
    copies = [
        pltpu.make_async_copy(
            p_hbm.at[pl.ds(i * span, span)], p_vmem.at[pl.ds(i * span, span)], sems.at[i]
        )
        for i in range(pieces)
    ]
    gram_copy = pltpu.make_async_copy(gram_any, gram_ref, gram_sem)
    gram_copy.start()
    for copy in copies:
        copy.start()
    density_columns(dens_ref, dcol)
    slots, live = rim_places(slot_ref[...], count_ref, elems)
    tile_dens = jnp.take_along_axis(rims(dcol, 1.0 / LANES), slots, axis=1) * live

    gram_copy.wait()
    row, col = iota((LANES, LANES), 0), iota((LANES, LANES), 1)
    packed = gram_ref[0:LANES, :]
    above = jnp.where(row < col, packed, 0.0)
    below = jnp.where(row > col, packed, 0.0)
    stiff = above + above.T + jnp.where(row == col, packed, 0.0)
    mass = below + below.T + jnp.where(row == col, gram_ref[LANES : LANES + 1, :], 0.0)
    inv_mass = invert_spd(mass)
    ritz_ref[0, 0] = jnp.sum(inv_mass * stiff) * (1.0 / LANES)
    half = jnp.dot(inv_mass, stiff, precision=HIGHEST, preferred_element_type=F32)
    sandwich = jnp.dot(half, inv_mass, precision=HIGHEST, preferred_element_type=F32)
    both[...] = jnp.zeros_like(both)
    both[0:LANES, 0:LANES] = inv_mass.astype(BF16)
    both[LANES:, LANES:] = sandwich.astype(BF16)

    per_piece = span * GROUP // STRIP
    for i in range(pieces):
        copies[i].wait()

        def body(it, _, i=i):
            unit = i * per_piece + it
            stiffs = p_vmem[pl.ds(unit * (STRIP // GROUP), STRIP // GROUP), 0:ROWS, :].reshape(STRIP // GROUP * ROWS, LANES)
            masses = p_vmem[pl.ds(unit * (STRIP // GROUP), STRIP // GROUP), ROWS:, :].reshape(STRIP // GROUP * ROWS, LANES)
            inner = jnp.dot(
                jnp.concatenate([stiffs, masses], axis=1), both[...], preferred_element_type=F32
            )
            part_stiff = (inner[:, :LANES] * stiffs.astype(F32)).reshape(STRIP // GROUP, 24, 8, LANES).sum(axis=1)
            part_mass = (inner[:, LANES:] * masses.astype(F32)).reshape(STRIP // GROUP, 24, 8, LANES).sum(axis=1)
            at = pl.ds(pl.multiple_of(unit * STRIP, STRIP), STRIP)
            dens = dcol[at, :]
            total[at, :] = 3.0 * dens * dens * part_stiff.reshape(STRIP, LANES) - part_mass.reshape(STRIP, LANES)
            return 0

        lax.fori_loop(0, per_piece, body, 0, unroll=12)

    for j in range(elems // LANES):
        block = total[pl.ds(j * LANES, LANES), :]
        sens_ref[j : j + 1, :] = jnp.sum(block.T, axis=0, keepdims=True) * scale
    tile_sens = jnp.take_along_axis(rims(total, scale), slots, axis=1) * live
    tiles = (live, tile_dens, tile_sens)
    for ref, directions in ((up_ref, (0, 2, 1)), (down_ref, (5, 7, 6)), (side_ref, (3, 4))):
        ref[...] = jnp.zeros_like(ref)
        for n, k in enumerate(directions):
            for ch, value in enumerate(tiles):
                ref[3 * n + ch : 3 * n + ch + 1, :] = value[k : k + 1]


def project_and_gram(connectivity, block_vectors, dens_rows, stiff_factor, mass_factor):
    elems = dens_rows.size
    groups = elems // GROUP
    steps = 9
    per_step = elems // UNIT // steps
    vmem = pl.BlockSpec(memory_space=pltpu.VMEM)
    smem = pl.BlockSpec(memory_space=pltpu.SMEM)
    return pl.pallas_call(
        lambda *refs: gram_kernel(elems, per_step, *refs),
        grid=(steps,),
        out_shape=(
            jax.ShapeDtypeStruct((groups, 2 * ROWS, LANES), BF16),
            jax.ShapeDtypeStruct((LANES + 8, LANES), F32),
        ),
        in_specs=[vmem] * 5,
        out_specs=(
            pl.BlockSpec((groups // steps, 2 * ROWS, LANES), lambda i: (i, 0, 0)),
            pl.BlockSpec((LANES + 8, LANES), lambda i: (0, 0)),
        ),
        scratch_shapes=[
            pltpu.VMEM((3 * elems + 24, LANES), F32),
            pltpu.VMEM((elems, LANES), F32),
            pltpu.VMEM((2 * ROWS, ROWS), BF16),
            pltpu.VMEM((8, elems), jnp.int32),
            pltpu.SMEM((8 * elems,), jnp.int32),
            pltpu.VMEM((UNIT // 16, ROWS, 2 * LANES), BF16),
            pltpu.VMEM((UNIT // 16, ROWS, 2 * LANES), BF16),
            pltpu.VMEM((4, UNIT // GROUP, ROWS, LANES), BF16),
            pltpu.VMEM((4, UNIT // GROUP, ROWS, LANES), BF16),
            pltpu.VMEM((2, LANES, LANES), F32),
            pltpu.SemaphoreType.DMA((8,)),
        ],
        compiler_params=pltpu.CompilerParams(vmem_limit_bytes=VMEM_LIMIT),
        name="gram",
    )(connectivity, block_vectors, dens_rows, stiff_factor, mass_factor)


def energies(scale, gram, proj, dens_rows, send_slot, send_count):
    elems = dens_rows.size
    groups = elems // GROUP
    vmem = pl.BlockSpec(memory_space=pltpu.VMEM)
    smem = pl.BlockSpec(memory_space=pltpu.SMEM)
    return pl.pallas_call(
        lambda *refs: energy_kernel(scale, *refs),
        out_shape=(
            jax.ShapeDtypeStruct((elems // LANES, LANES), F32),
            jax.ShapeDtypeStruct((16, LANES), F32),
            jax.ShapeDtypeStruct((16, LANES), F32),
            jax.ShapeDtypeStruct((8, LANES), F32),
            jax.ShapeDtypeStruct((1, 1), F32),
        ),
        in_specs=[pl.BlockSpec(memory_space=pl.ANY)] * 2 + [vmem, vmem, smem],
        out_specs=(vmem,) * 4 + (smem,),
        scratch_shapes=[
            pltpu.VMEM((LANES + 8, LANES), F32),
            pltpu.VMEM((groups, 2 * ROWS, LANES), BF16),
            pltpu.VMEM((elems, LANES), F32),
            pltpu.VMEM((2 * LANES, 2 * LANES), BF16),
            pltpu.VMEM((elems, LANES), F32),
            pltpu.SemaphoreType.DMA,
            pltpu.SemaphoreType.DMA((6,)),
        ],
        compiler_params=pltpu.CompilerParams(vmem_limit_bytes=VMEM_LIMIT),
        name="energy",
    )(gram, proj, dens_rows, send_slot, send_count)


def split3(value):
    high = value.astype(BF16)
    rest = value - high.astype(F32)
    mid = rest.astype(BF16)
    low = (rest - mid.astype(F32)).astype(BF16)
    return high, mid, low


def owner_kernel(
    up_any, down_any, left_any, right_any, target_ref, weight_ref, dens_ref, sens_ref, fdens_ref, fsens_ref,
    up_ref, down_ref, left_ref, right_ref, sems
):
    pairs = ((up_any, up_ref), (down_any, down_ref), (left_any, left_ref), (right_any, right_ref))
    copies = [pltpu.make_async_copy(src, dst, sems.at[i]) for i, (src, dst) in enumerate(pairs)]
    for copy in copies:
        copy.start()
    lane = iota((1, LANES), 1)

    def lanes_of(main, corner):
        return jnp.where(lane < 96, main, pltpu.roll(corner, 96, 1))

    def by_side(table):
        table = jnp.concatenate([table, jnp.zeros((8, LANES - table.shape[1]), table.dtype)], axis=1)
        pairs = ((1, 0), (6, 5), (3, 2), (4, 7))
        return [lanes_of(table[m : m + 1], table[c : c + 1]) for m, c in pairs]

    weights = by_side(weight_ref[...])
    targets = jnp.concatenate(by_side(target_ref[...]), axis=1)
    for copy in copies:
        copy.wait()
    values = [[], [], []]
    for ch in range(3):

        def at(ref, first):
            return ref[first + ch : first + ch + 1, :]

        sides = (
            lanes_of(at(up_ref, 6), at(left_ref, 8)),
            lanes_of(at(down_ref, 6), at(left_ref, 16)),
            lanes_of(at(left_ref, 0), at(right_ref, 11)),
            lanes_of(at(right_ref, 3), at(right_ref, 19)),
        )
        for side in range(4):
            values[ch].append(sides[side] * weights[side])
    stacked = jnp.concatenate([jnp.concatenate(v, axis=1) for v in values], axis=0)
    high, mid, low = split3(stacked)
    left = jnp.concatenate([high, mid, low, jnp.zeros((7, 4 * LANES), BF16)], axis=0)
    last = dens_ref.shape[0] - 1
    for j in range(last + 1):
        part = slice(0 if j in (0, last) else 2 * LANES, 4 * LANES)
        hit = targets[:, part] == iota((LANES, part.stop - part.start), 0) + j * LANES
        hot = jnp.where(hit, 1.0, 0.0).astype(BF16)
        sums = lax.dot_general(left[:, part], hot, (((1,), (1,)), ((), ())), preferred_element_type=F32)
        sums = sums[0:3] + sums[3:6] + sums[6:9]
        under = 1.0 + sums[0:1]
        fdens_ref[j : j + 1, :] = (dens_ref[j : j + 1, :] + sums[1:2]) / under
        fsens_ref[j : j + 1, :] = (sens_ref[j : j + 1, :] + sums[2:3]) / under


def place(index, sizes):
    rows, cols = sizes
    return [index // cols // 2, index // cols % 2, index % cols // 4, index % 4]


def swapped(sizes, axis, step):
    rows, cols = sizes
    lengths = [rows // 2, 2, cols // 4, 4]
    pairs = []
    for i in range(rows * cols):
        at = place(i, sizes)
        at[axis] = (at[axis] + step) % lengths[axis]
        pairs.append((i, ((at[0] * 2 + at[1]) * lengths[2] + at[2]) * 4 + at[3]))
    return pairs


def sum_over_devices(value, sizes):
    value = value + lax.ppermute(value, AXES, swapped(sizes, 1, 1))
    lengths = [sizes[0] // 2, 2, sizes[1] // 4, 4]
    for axis in (3, 2, 0):
        others = [lax.ppermute(value, AXES, swapped(sizes, axis, s)) for s in range(1, lengths[axis])]
        for other in others:
            value = value + other
    return value


def torus(axis, step):
    size = lax.axis_size(axis)
    return [(i, (i + step) % size) for i in range(size)]


def per_device(
    block_vectors, connectivity, density, stiff_factor, mass_factor, send_slot, send_count, recv_target, recv_weight
):
    vec_count = block_vectors.shape[1]
    elems = density.shape[0]
    sizes = (lax.axis_size("gx"), lax.axis_size("gy"))
    scale = float(elems * sizes[0] * sizes[1]) / vec_count

    dens_rows = density.reshape(elems // LANES, LANES)

    proj, gram = project_and_gram(connectivity, block_vectors, dens_rows, stiff_factor, mass_factor)
    gram = sum_over_devices(gram, sizes)

    sens_rows, up, down, side, ritz = energies(scale, gram, proj, dens_rows, send_slot[0], send_count)

    up = lax.ppermute(up, "gx", torus("gx", -1))
    down = lax.ppermute(down, "gx", torus("gx", 1))
    packet = jnp.concatenate([side, up[:8], down[:8]], axis=0)
    left = lax.ppermute(packet, "gy", torus("gy", -1))
    right = lax.ppermute(packet, "gy", torus("gy", 1))

    vmem = pl.BlockSpec(memory_space=pltpu.VMEM)
    fdens, fsens = pl.pallas_call(
        owner_kernel,
        out_shape=(jax.ShapeDtypeStruct((elems // LANES, LANES), F32),) * 2,
        in_specs=[pl.BlockSpec(memory_space=pl.ANY)] * 4 + [vmem] * 4,
        out_specs=(vmem, vmem),
        scratch_shapes=[
            pltpu.VMEM((16, LANES), F32),
            pltpu.VMEM((16, LANES), F32),
            pltpu.VMEM((24, LANES), F32),
            pltpu.VMEM((24, LANES), F32),
            pltpu.SemaphoreType.DMA((4,)),
        ],
        name="owner",
    )(up, down, left, right, recv_target[0], recv_weight[0], dens_rows, sens_rows)
    return fdens.reshape(elems), fsens.reshape(elems), ritz.reshape(())


def solution(mesh):
    placed = (
        P(None, None, ("gx", "gy")),
        P(None, ("gx", "gy")),
        P(("gx", "gy")),
        P(),
        P(),
        P(("gx", "gy"), None, None),
        P(("gx", "gy"), None),
        P(("gx", "gy"), None, None),
        P(("gx", "gy"), None, None),
    )
    return jax.shard_map(
        per_device,
        mesh=mesh,
        in_specs=placed,
        out_specs=(P(("gx", "gy")), P(("gx", "gy")), P()),
        check_vma=False,
    )
```

```python
import jax
import jax.numpy as jnp
from jax import lax
from jax.experimental import pallas as pl
from jax.experimental.pallas import tpu as pltpu
from jax.sharding import PartitionSpec as P

SIDE = 48
RIM = 2
LANES = 128
GROUP = 8
UNIT = 128
STRIP = 32
ROWS = 24 * GROUP
AXES = ("gx", "gy")
MIB = 1024 * 1024
F32 = jnp.float32
BF16 = jnp.bfloat16
HIGHEST = lax.Precision.HIGHEST


def iota(shape, dim):
    return lax.broadcasted_iota(jnp.int32, shape, dim)


def density_columns(dens_ref, dcol):
    for j in range(dens_ref.shape[0]):
        row = jnp.broadcast_to(dens_ref[j : j + 1, :], (LANES, LANES))
        dcol[pl.ds(j * LANES, LANES), :] = row.T


PIECES = (
    ((0, 0), (1, 3), (2, 6)),
    ((2, -2), (3, 1), (4, 4), (5, 7)),
    ((5, -1), (6, 2), (7, 5)),
)


def spread(factor):
    dofs = factor.shape[0]
    wide, tall = (ROWS, dofs), (dofs, ROWS)
    take_row = (iota(wide, 0) >> 3) == iota(wide, 1)
    out = iota(tall, 1)
    within = lax.rem(out, dofs)
    corner = within // 3
    take_col = (within - 3 * corner) * 8 + corner == iota(tall, 0)
    picked = jnp.dot(jnp.where(take_row, 1.0, 0.0).astype(BF16), factor, preferred_element_type=F32)
    full = jnp.dot(picked.astype(BF16), jnp.where(take_col, 1.0, 0.0).astype(BF16), preferred_element_type=F32)
    square = (ROWS, ROWS)
    same = (iota(square, 0) & 7) == iota(square, 1) // dofs
    return jnp.where(same, full, 0.0).astype(BF16)


def gram_kernel(
    elems, per_step, conn_ref, vec_ref, dens_ref, stiff_ref, mass_ref, p_ref, out_ref,
    table, dcol, w_ref, tripled, rows_smem, x_even, x_odd, k_even, k_odd, acc, sem
):
    step = pl.program_id(0)
    units = elems // UNIT
    sub = iota((8, LANES), 0)

    def gather(unit, xbuf, qs=tuple(range(UNIT // 16))):
        base = unit * UNIT
        for q in qs:
            for h in range(2):
                for pair in range(4):
                    regs = []
                    for e in range(2):
                        at = base + (q * 16 + h * 8 + pair * 2 + e)
                        rows = [rows_smem[a * elems + at] for a in range(8)]
                        for pieces in PIECES:
                            value = None
                            for corner, first in pieces:
                                got = table[pl.ds(rows[corner] + (8 - first), 8), :]
                                value = got if value is None else jnp.where(sub >= first, got, value)
                            regs.append(value)
                    block = jnp.concatenate(regs, axis=0).astype(BF16)
                    xbuf[q, pl.ds(pair * 48, 48), pl.ds(h * LANES, LANES)] = block

    @pl.when(step == 0)
    def _():
        tripled[...] = conn_ref[...] * 3
        copies = [
            pltpu.make_async_copy(tripled.at[a], rows_smem.at[pl.ds(a * elems, elems)], sem.at[a]) for a in range(8)
        ]
        for copy in copies:
            copy.start()
        w_ref[0:ROWS] = spread(stiff_ref[...])
        w_ref[ROWS:] = spread(mass_ref[...])
        for c in range(3):
            for j in range(elems // LANES):
                block = vec_ref[c, :, pl.ds(j * LANES, LANES)].astype(F32).T
                table[pl.ds(8 + 3 * LANES * j + c, LANES, stride=3), :] = block
        density_columns(dens_ref, dcol)
        acc[...] = jnp.zeros_like(acc)
        k_odd[...] = jnp.zeros_like(k_odd)
        for copy in copies:
            copy.wait()
        gather(0, x_even)

    def project(unit, local, xbuf, kept, qs):
        for q in qs:
            full = jnp.dot(w_ref[...], xbuf[q], preferred_element_type=F32).astype(BF16)
            for h in range(2):
                part = full[:, h * LANES : (h + 1) * LANES]
                chunk = 2 * q + h
                p_ref[local * (UNIT // GROUP) + chunk] = part
                wide = part.astype(F32).reshape(2, 24, 8, LANES)
                dens = dcol[pl.ds(pl.multiple_of(unit * UNIT + chunk * 8, 8), 8), :]
                for kind, factor in enumerate((dens * dens * dens, dens)):
                    kept[kind, chunk] = part[kind * ROWS : (kind + 1) * ROWS]
                    kept[2 + kind, chunk] = (wide[kind] * factor[None]).reshape(ROWS, LANES).astype(BF16)

    def add_grams(kept):
        left = jnp.concatenate([kept[2 + kind].reshape(UNIT // GROUP * ROWS, LANES) for kind in range(2)], axis=1)
        right = jnp.concatenate([kept[kind].reshape(UNIT // GROUP * ROWS, LANES) for kind in range(2)], axis=1)
        full = lax.dot_general(left, right, (((0,), (0,)), ((), ())), preferred_element_type=F32)
        acc[0] += full[:LANES, :LANES]
        acc[1] += full[LANES:, LANES:]

    def body(it, _):
        unit = step * per_step + 2 * it
        for q in range(UNIT // 16):
            gather(unit + 1, x_odd, (q,))
            project(unit, 2 * it, x_even, k_even, (q,))
        add_grams(k_odd)
        after = jnp.minimum(unit + 2, units - 1)
        for q in range(UNIT // 16):
            gather(after, x_even, (q,))
            project(unit + 1, 2 * it + 1, x_odd, k_odd, (q,))
        add_grams(k_even)
        return 0

    lax.fori_loop(0, per_step // 2, body, 0)

    @pl.when(step == pl.num_programs(0) - 1)
    def _():
        add_grams(k_odd)
        stiff = 0.5 * (acc[0] + acc[0].T)
        mass = 0.5 * (acc[1] + acc[1].T)
        row, col = iota((LANES, LANES), 0), iota((LANES, LANES), 1)
        out_ref[0:LANES, :] = jnp.where(row <= col, stiff, mass)
        diag = jnp.sum(jnp.where(row == col, mass, 0.0), axis=0, keepdims=True)
        out_ref[LANES : LANES + 8, :] = jnp.broadcast_to(diag, (8, LANES))


def invert_spd(gram):
    lane = iota((8, LANES), 1)
    sub = iota((8, LANES), 0)

    def column(reg, k):
        return jnp.broadcast_to(reg[:, k : k + 1], (8, LANES))

    def row(reg, k):
        return jnp.broadcast_to(reg[k : k + 1, :], (8, LANES))

    regs = [gram[8 * g : 8 * g + 8, :] for g in range(LANES // 8)]
    for own in range(LANES // 8):
        first = 8 * own
        inside = (lane >= first) & (lane < first + 8)
        cols = [[column(reg, first + j) for j in range(8)] for reg in regs]
        held = list(cols[own])
        panel = jnp.where(inside, jnp.where(lane == first + sub, 1.0, 0.0), regs[own])
        for k in range(8):
            inverse = 1.0 / row(held[k], k)
            here = sub == k
            for at in range(k + 1, 9):
                value = held[at] if at < 8 else panel
                pivot = row(value, k)
                value = jnp.where(here, 0.0, value) - jnp.where(here, -pivot, held[k] * pivot) * inverse
                if at < 8:
                    held[at] = value
                else:
                    panel = value
        rows = [row(panel, j) for j in range(8)]
        for g in range(LANES // 8):
            if g == own:
                regs[g] = panel
                continue
            value = jnp.where(inside, 0.0, regs[g])
            for j in range(8):
                value = value - cols[g][j] * rows[j]
            regs[g] = value
    return jnp.concatenate(regs, axis=0)


def rims(column, scale):
    elems = column.shape[0]

    def summed(rows):
        return jnp.sum(rows.T, axis=0, keepdims=True) * scale

    def side(first):
        parts = [column[pl.ds(first + c, SIDE, stride=SIDE), :] for c in range(RIM)]
        parts.append(jnp.zeros((LANES - RIM * SIDE, LANES), F32))
        return summed(jnp.concatenate(parts, axis=0))

    top = summed(column[pl.ds(0, LANES), :])
    bottom = summed(column[pl.ds(elems - LANES, LANES), :])
    left, right = side(0), side(SIDE - RIM)
    return jnp.concatenate([top, top, top, left, right, bottom, bottom, bottom], axis=0)


def rim_places(slots, count_ref, elems):
    slots = jnp.concatenate([slots, jnp.zeros((8, LANES - slots.shape[1]), jnp.int32)], axis=1)
    lane = iota((1, LANES), 1)
    row = slots // SIDE
    col = slots - row * SIDE
    k = iota(slots.shape, 0)
    across = jnp.where(k == 3, col, col - (SIDE - RIM)) * SIDE + row
    place = jnp.where(k < 3, slots, jnp.where(k < 5, across, slots - (elems - LANES)))
    live = jnp.concatenate([jnp.where(lane < count_ref[0, d], 1.0, 0.0) for d in range(8)], axis=0)
    return jnp.where(live > 0.0, place, 0), live


def energy_kernel(
    scale, gram_any, p_hbm, dens_ref, slot_ref, count_ref, sens_ref, up_ref, down_ref, side_ref, ritz_ref,
    gram_ref, p_vmem, dcol, both, total, gram_sem, sems
):
    elems = dcol.shape[0]
    groups = elems // GROUP
    pieces = sems.shape[0]
    span = groups // pieces
    copies = [
        pltpu.make_async_copy(
            p_hbm.at[pl.ds(i * span, span)], p_vmem.at[pl.ds(i * span, span)], sems.at[i]
        )
        for i in range(pieces)
    ]
    gram_copy = pltpu.make_async_copy(gram_any, gram_ref, gram_sem)
    gram_copy.start()
    for copy in copies:
        copy.start()
    density_columns(dens_ref, dcol)
    slots, live = rim_places(slot_ref[...], count_ref, elems)
    tile_dens = jnp.take_along_axis(rims(dcol, 1.0 / LANES), slots, axis=1) * live

    gram_copy.wait()
    row, col = iota((LANES, LANES), 0), iota((LANES, LANES), 1)
    packed = gram_ref[0:LANES, :]
    above = jnp.where(row < col, packed, 0.0)
    below = jnp.where(row > col, packed, 0.0)
    stiff = above + above.T + jnp.where(row == col, packed, 0.0)
    mass = below + below.T + jnp.where(row == col, gram_ref[LANES : LANES + 1, :], 0.0)
    inv_mass = invert_spd(mass)
    ritz_ref[0, 0] = jnp.sum(inv_mass * stiff) * (1.0 / LANES)
    half = jnp.dot(inv_mass, stiff, precision=HIGHEST, preferred_element_type=F32)
    sandwich = jnp.dot(half, inv_mass, precision=HIGHEST, preferred_element_type=F32)
    both[...] = jnp.zeros_like(both)
    both[0:LANES, 0:LANES] = inv_mass.astype(BF16)
    both[LANES:, LANES:] = sandwich.astype(BF16)

    per_piece = span * GROUP // STRIP
    for i in range(pieces):
        copies[i].wait()

        def body(it, _, i=i):
            unit = i * per_piece + it
            stiffs = p_vmem[pl.ds(unit * (STRIP // GROUP), STRIP // GROUP), 0:ROWS, :].reshape(STRIP // GROUP * ROWS, LANES)
            masses = p_vmem[pl.ds(unit * (STRIP // GROUP), STRIP // GROUP), ROWS:, :].reshape(STRIP // GROUP * ROWS, LANES)
            inner = jnp.dot(
                jnp.concatenate([stiffs, masses], axis=1), both[...], preferred_element_type=F32
            )
            part_stiff = (inner[:, :LANES] * stiffs.astype(F32)).reshape(STRIP // GROUP, 24, 8, LANES).sum(axis=1)
            part_mass = (inner[:, LANES:] * masses.astype(F32)).reshape(STRIP // GROUP, 24, 8, LANES).sum(axis=1)
            at = pl.ds(pl.multiple_of(unit * STRIP, STRIP), STRIP)
            dens = dcol[at, :]
            total[at, :] = 3.0 * dens * dens * part_stiff.reshape(STRIP, LANES) - part_mass.reshape(STRIP, LANES)
            return 0

        lax.fori_loop(0, per_piece, body, 0, unroll=12)

    for j in range(elems // LANES):
        block = total[pl.ds(j * LANES, LANES), :]
        sens_ref[j : j + 1, :] = jnp.sum(block.T, axis=0, keepdims=True) * scale
    tile_sens = jnp.take_along_axis(rims(total, scale), slots, axis=1) * live
    tiles = (live, tile_dens, tile_sens)
    for ref, directions in ((up_ref, (0, 2, 1)), (down_ref, (5, 7, 6)), (side_ref, (3, 4))):
        ref[...] = jnp.zeros_like(ref)
        for n, k in enumerate(directions):
            for ch, value in enumerate(tiles):
                ref[3 * n + ch : 3 * n + ch + 1, :] = value[k : k + 1]


def project_and_gram(connectivity, block_vectors, dens_rows, stiff_factor, mass_factor):
    elems = dens_rows.size
    groups = elems // GROUP
    steps = 9
    per_step = elems // UNIT // steps
    vmem = pl.BlockSpec(memory_space=pltpu.VMEM)
    smem = pl.BlockSpec(memory_space=pltpu.SMEM)
    return pl.pallas_call(
        lambda *refs: gram_kernel(elems, per_step, *refs),
        grid=(steps,),
        out_shape=(
            jax.ShapeDtypeStruct((groups, 2 * ROWS, LANES), BF16),
            jax.ShapeDtypeStruct((LANES + 8, LANES), F32),
        ),
        in_specs=[vmem] * 5,
        out_specs=(
            pl.BlockSpec((groups // steps, 2 * ROWS, LANES), lambda i: (i, 0, 0)),
            pl.BlockSpec((LANES + 8, LANES), lambda i: (0, 0)),
        ),
        scratch_shapes=[
            pltpu.VMEM((3 * elems + 24, LANES), F32),
            pltpu.VMEM((elems, LANES), F32),
            pltpu.VMEM((2 * ROWS, ROWS), BF16),
            pltpu.VMEM((8, elems), jnp.int32),
            pltpu.SMEM((8 * elems,), jnp.int32),
            pltpu.VMEM((UNIT // 16, ROWS, 2 * LANES), BF16),
            pltpu.VMEM((UNIT // 16, ROWS, 2 * LANES), BF16),
            pltpu.VMEM((4, UNIT // GROUP, ROWS, LANES), BF16),
            pltpu.VMEM((4, UNIT // GROUP, ROWS, LANES), BF16),
            pltpu.VMEM((2, LANES, LANES), F32),
            pltpu.SemaphoreType.DMA((8,)),
        ],
        compiler_params=pltpu.CompilerParams(vmem_limit_bytes=60 * MIB),
        name="gram",
    )(connectivity, block_vectors, dens_rows, stiff_factor, mass_factor)


def energies(scale, gram, proj, dens_rows, send_slot, send_count):
    elems = dens_rows.size
    groups = elems // GROUP
    vmem = pl.BlockSpec(memory_space=pltpu.VMEM)
    smem = pl.BlockSpec(memory_space=pltpu.SMEM)
    return pl.pallas_call(
        lambda *refs: energy_kernel(scale, *refs),
        out_shape=(
            jax.ShapeDtypeStruct((elems // LANES, LANES), F32),
            jax.ShapeDtypeStruct((16, LANES), F32),
            jax.ShapeDtypeStruct((16, LANES), F32),
            jax.ShapeDtypeStruct((8, LANES), F32),
            jax.ShapeDtypeStruct((1, 1), F32),
        ),
        in_specs=[pl.BlockSpec(memory_space=pl.ANY)] * 2 + [vmem, vmem, smem],
        out_specs=(vmem,) * 4 + (smem,),
        scratch_shapes=[
            pltpu.VMEM((LANES + 8, LANES), F32),
            pltpu.VMEM((groups, 2 * ROWS, LANES), BF16),
            pltpu.VMEM((elems, LANES), F32),
            pltpu.VMEM((2 * LANES, 2 * LANES), BF16),
            pltpu.VMEM((elems, LANES), F32),
            pltpu.SemaphoreType.DMA,
            pltpu.SemaphoreType.DMA((6,)),
        ],
        compiler_params=pltpu.CompilerParams(vmem_limit_bytes=44 * MIB),
        name="energy",
    )(gram, proj, dens_rows, send_slot, send_count)


def split3(value):
    high = value.astype(BF16)
    rest = value - high.astype(F32)
    mid = rest.astype(BF16)
    low = (rest - mid.astype(F32)).astype(BF16)
    return high, mid, low


def owner_kernel(
    up_any, down_any, left_any, right_any, target_ref, weight_ref, dens_ref, sens_ref, fdens_ref, fsens_ref,
    up_ref, down_ref, left_ref, right_ref, sems
):
    pairs = ((up_any, up_ref), (down_any, down_ref), (left_any, left_ref), (right_any, right_ref))
    copies = [pltpu.make_async_copy(src, dst, sems.at[i]) for i, (src, dst) in enumerate(pairs)]
    for copy in copies:
        copy.start()
    lane = iota((1, LANES), 1)

    def lanes_of(main, corner):
        return jnp.where(lane < 96, main, pltpu.roll(corner, 96, 1))

    def by_side(table):
        table = jnp.concatenate([table, jnp.zeros((8, LANES - table.shape[1]), table.dtype)], axis=1)
        pairs = ((1, 0), (6, 5), (3, 2), (4, 7))
        return [lanes_of(table[m : m + 1], table[c : c + 1]) for m, c in pairs]

    weights = by_side(weight_ref[...])
    targets = jnp.concatenate(by_side(target_ref[...]), axis=1)
    for copy in copies:
        copy.wait()
    values = [[], [], []]
    for ch in range(3):

        def at(ref, first):
            return ref[first + ch : first + ch + 1, :]

        sides = (
            lanes_of(at(up_ref, 6), at(left_ref, 8)),
            lanes_of(at(down_ref, 6), at(left_ref, 16)),
            lanes_of(at(left_ref, 0), at(right_ref, 11)),
            lanes_of(at(right_ref, 3), at(right_ref, 19)),
        )
        for side in range(4):
            values[ch].append(sides[side] * weights[side])
    stacked = jnp.concatenate([jnp.concatenate(v, axis=1) for v in values], axis=0)
    high, mid, low = split3(stacked)
    left = jnp.concatenate([high, mid, low, jnp.zeros((7, 4 * LANES), BF16)], axis=0)
    last = dens_ref.shape[0] - 1
    for j in range(last + 1):
        part = slice(0 if j in (0, last) else 2 * LANES, 4 * LANES)
        hit = targets[:, part] == iota((LANES, part.stop - part.start), 0) + j * LANES
        hot = jnp.where(hit, 1.0, 0.0).astype(BF16)
        sums = lax.dot_general(left[:, part], hot, (((1,), (1,)), ((), ())), preferred_element_type=F32)
        sums = sums[0:3] + sums[3:6] + sums[6:9]
        under = 1.0 + sums[0:1]
        fdens_ref[j : j + 1, :] = (dens_ref[j : j + 1, :] + sums[1:2]) / under
        fsens_ref[j : j + 1, :] = (sens_ref[j : j + 1, :] + sums[2:3]) / under


def place(index, sizes):
    rows, cols = sizes
    return [index // cols // 2, index // cols % 2, index % cols // 4, index % 4]


def swapped(sizes, axis, step):
    rows, cols = sizes
    lengths = [rows // 2, 2, cols // 4, 4]
    pairs = []
    for i in range(rows * cols):
        at = place(i, sizes)
        at[axis] = (at[axis] + step) % lengths[axis]
        pairs.append((i, ((at[0] * 2 + at[1]) * lengths[2] + at[2]) * 4 + at[3]))
    return pairs


def sum_over_devices(value, sizes):
    value = value + lax.ppermute(value, AXES, swapped(sizes, 1, 1))
    lengths = [sizes[0] // 2, 2, sizes[1] // 4, 4]
    for axis in (3, 2, 0):
        others = [lax.ppermute(value, AXES, swapped(sizes, axis, s)) for s in range(1, lengths[axis])]
        for other in others:
            value = value + other
    return value


def torus(axis, step):
    size = lax.axis_size(axis)
    return [(i, (i + step) % size) for i in range(size)]


def per_device(
    block_vectors, connectivity, density, stiff_factor, mass_factor, send_slot, send_count, recv_target, recv_weight
):
    vec_count = block_vectors.shape[1]
    elems = density.shape[0]
    sizes = (lax.axis_size("gx"), lax.axis_size("gy"))
    scale = float(elems * sizes[0] * sizes[1]) / vec_count

    dens_rows = density.reshape(elems // LANES, LANES)

    proj, gram = project_and_gram(connectivity, block_vectors, dens_rows, stiff_factor, mass_factor)
    gram = sum_over_devices(gram, sizes)

    sens_rows, up, down, side, ritz = energies(scale, gram, proj, dens_rows, send_slot[0], send_count)

    up = lax.ppermute(up, "gx", torus("gx", -1))
    down = lax.ppermute(down, "gx", torus("gx", 1))
    packet = jnp.concatenate([side, up[:8], down[:8]], axis=0)
    left = lax.ppermute(packet, "gy", torus("gy", -1))
    right = lax.ppermute(packet, "gy", torus("gy", 1))

    vmem = pl.BlockSpec(memory_space=pltpu.VMEM)
    fdens, fsens = pl.pallas_call(
        owner_kernel,
        out_shape=(jax.ShapeDtypeStruct((elems // LANES, LANES), F32),) * 2,
        in_specs=[pl.BlockSpec(memory_space=pl.ANY)] * 4 + [vmem] * 4,
        out_specs=(vmem, vmem),
        scratch_shapes=[
            pltpu.VMEM((16, LANES), F32),
            pltpu.VMEM((16, LANES), F32),
            pltpu.VMEM((24, LANES), F32),
            pltpu.VMEM((24, LANES), F32),
            pltpu.SemaphoreType.DMA((4,)),
        ],
        compiler_params=pltpu.CompilerParams(vmem_limit_bytes=8 * MIB),
        name="owner",
    )(up, down, left, right, recv_target[0], recv_weight[0], dens_rows, sens_rows)
    return fdens.reshape(elems), fsens.reshape(elems), ritz.reshape(())


def solution(mesh):
    placed = (
        P(None, None, ("gx", "gy")),
        P(None, ("gx", "gy")),
        P(("gx", "gy")),
        P(),
        P(),
        P(("gx", "gy"), None, None),
        P(("gx", "gy"), None),
        P(("gx", "gy"), None, None),
        P(("gx", "gy"), None, None),
    )
    return jax.shard_map(
        per_device,
        mesh=mesh,
        in_specs=placed,
        out_specs=(P(("gx", "gy")), P(("gx", "gy")), P()),
        check_vma=False,
    )
```

```python
import jax
import jax.numpy as jnp
from jax import lax
from jax.experimental import pallas as pl
from jax.experimental.pallas import tpu as pltpu
from jax.sharding import PartitionSpec as P

SIDE = 48
RIM = 2
LANES = 128
GROUP = 8
UNIT = 128
STRIP = 32
ROWS = 24 * GROUP
AXES = ("gx", "gy")
MIB = 1024 * 1024
F32 = jnp.float32
BF16 = jnp.bfloat16
HIGHEST = lax.Precision.HIGHEST


def iota(shape, dim):
    return lax.broadcasted_iota(jnp.int32, shape, dim)


def density_columns(dens_ref, dcol):
    for j in range(dens_ref.shape[0]):
        row = jnp.broadcast_to(dens_ref[j : j + 1, :], (LANES, LANES))
        dcol[pl.ds(j * LANES, LANES), :] = row.T


PIECES = (
    ((0, 0), (1, 3), (2, 6)),
    ((2, -2), (3, 1), (4, 4), (5, 7)),
    ((5, -1), (6, 2), (7, 5)),
)


def spread(factor):
    dofs = factor.shape[0]
    wide, tall = (ROWS, dofs), (dofs, ROWS)
    take_row = (iota(wide, 0) >> 3) == iota(wide, 1)
    out = iota(tall, 1)
    within = lax.rem(out, dofs)
    corner = within // 3
    take_col = (within - 3 * corner) * 8 + corner == iota(tall, 0)
    picked = jnp.dot(jnp.where(take_row, 1.0, 0.0).astype(BF16), factor, preferred_element_type=F32)
    full = jnp.dot(picked.astype(BF16), jnp.where(take_col, 1.0, 0.0).astype(BF16), preferred_element_type=F32)
    square = (ROWS, ROWS)
    same = (iota(square, 0) & 7) == iota(square, 1) // dofs
    return jnp.where(same, full, 0.0).astype(BF16)


def gram_kernel(
    elems, per_step, conn_ref, vec_ref, dens_ref, stiff_ref, mass_ref, p_ref, out_ref,
    table, dcol, w_ref, tripled, rows_smem, x_even, x_odd, k_even, k_odd, acc, sem
):
    step = pl.program_id(0)
    units = elems // UNIT
    sub = iota((8, LANES), 0)

    def gather(unit, xbuf, qs=tuple(range(UNIT // 16))):
        base = unit * UNIT
        for q in qs:
            for h in range(2):
                for pair in range(4):
                    regs = []
                    for e in range(2):
                        at = base + (q * 16 + h * 8 + pair * 2 + e)
                        rows = [rows_smem[a * elems + at] for a in range(8)]
                        for pieces in PIECES:
                            value = None
                            for corner, first in pieces:
                                got = table[pl.ds(rows[corner] + (8 - first), 8), :]
                                value = got if value is None else jnp.where(sub >= first, got, value)
                            regs.append(value)
                    block = jnp.concatenate(regs, axis=0).astype(BF16)
                    xbuf[q, pl.ds(pair * 48, 48), pl.ds(h * LANES, LANES)] = block

    @pl.when(step == 0)
    def _():
        tripled[...] = conn_ref[...] * 3
        copies = [
            pltpu.make_async_copy(tripled.at[a], rows_smem.at[pl.ds(a * elems, elems)], sem.at[a]) for a in range(8)
        ]
        for copy in copies:
            copy.start()
        w_ref[0:ROWS] = spread(stiff_ref[...])
        w_ref[ROWS:] = spread(mass_ref[...])
        for c in range(3):
            for j in range(elems // LANES):
                block = vec_ref[c, :, pl.ds(j * LANES, LANES)].astype(F32).T
                table[pl.ds(8 + 3 * LANES * j + c, LANES, stride=3), :] = block
        density_columns(dens_ref, dcol)
        acc[...] = jnp.zeros_like(acc)
        k_odd[...] = jnp.zeros_like(k_odd)
        for copy in copies:
            copy.wait()
        gather(0, x_even)

    def project(unit, local, xbuf, kept, qs):
        for q in qs:
            full = jnp.dot(w_ref[...], xbuf[q], preferred_element_type=F32).astype(BF16)
            for h in range(2):
                part = full[:, h * LANES : (h + 1) * LANES]
                chunk = 2 * q + h
                p_ref[local * (UNIT // GROUP) + chunk] = part
                wide = part.astype(F32).reshape(2, 24, 8, LANES)
                dens = dcol[pl.ds(pl.multiple_of(unit * UNIT + chunk * 8, 8), 8), :]
                for kind, factor in enumerate((dens * dens * dens, dens)):
                    kept[kind, chunk] = part[kind * ROWS : (kind + 1) * ROWS]
                    kept[2 + kind, chunk] = (wide[kind] * factor[None]).reshape(ROWS, LANES).astype(BF16)

    def add_grams(kept):
        left = jnp.concatenate([kept[2 + kind].reshape(UNIT // GROUP * ROWS, LANES) for kind in range(2)], axis=1)
        right = jnp.concatenate([kept[kind].reshape(UNIT // GROUP * ROWS, LANES) for kind in range(2)], axis=1)
        full = lax.dot_general(left, right, (((0,), (0,)), ((), ())), preferred_element_type=F32)
        acc[0] += full[:LANES, :LANES]
        acc[1] += full[LANES:, LANES:]

    def body(it, _):
        unit = step * per_step + 2 * it
        for q in range(UNIT // 16):
            gather(unit + 1, x_odd, (q,))
            project(unit, 2 * it, x_even, k_even, (q,))
        add_grams(k_odd)
        after = jnp.minimum(unit + 2, units - 1)
        for q in range(UNIT // 16):
            gather(after, x_even, (q,))
            project(unit + 1, 2 * it + 1, x_odd, k_odd, (q,))
        add_grams(k_even)
        return 0

    lax.fori_loop(0, per_step // 2, body, 0)

    @pl.when(step == pl.num_programs(0) - 1)
    def _():
        add_grams(k_odd)
        stiff = 0.5 * (acc[0] + acc[0].T)
        mass = 0.5 * (acc[1] + acc[1].T)
        row, col = iota((LANES, LANES), 0), iota((LANES, LANES), 1)
        out_ref[0:LANES, :] = jnp.where(row <= col, stiff, mass)
        diag = jnp.sum(jnp.where(row == col, mass, 0.0), axis=0, keepdims=True)
        out_ref[LANES : LANES + 8, :] = jnp.broadcast_to(diag, (8, LANES))


def invert_spd(gram):
    lane = iota((8, LANES), 1)
    sub = iota((8, LANES), 0)

    def column(reg, k):
        return jnp.broadcast_to(reg[:, k : k + 1], (8, LANES))

    def row(reg, k):
        return jnp.broadcast_to(reg[k : k + 1, :], (8, LANES))

    regs = [gram[8 * g : 8 * g + 8, :] for g in range(LANES // 8)]
    for own in range(LANES // 8):
        first = 8 * own
        inside = (lane >= first) & (lane < first + 8)
        cols = [[column(reg, first + j) for j in range(8)] for reg in regs]
        held = list(cols[own])
        panel = jnp.where(inside, jnp.where(lane == first + sub, 1.0, 0.0), regs[own])
        for k in range(8):
            inverse = 1.0 / row(held[k], k)
            here = sub == k
            for at in range(k + 1, 9):
                value = held[at] if at < 8 else panel
                pivot = row(value, k)
                value = jnp.where(here, 0.0, value) - jnp.where(here, -pivot, held[k] * pivot) * inverse
                if at < 8:
                    held[at] = value
                else:
                    panel = value
        rows = [row(panel, j) for j in range(8)]
        for g in range(LANES // 8):
            if g == own:
                regs[g] = panel
                continue
            value = jnp.where(inside, 0.0, regs[g])
            for j in range(8):
                value = value - cols[g][j] * rows[j]
            regs[g] = value
    return jnp.concatenate(regs, axis=0)


def rims(column, scale):
    elems = column.shape[0]

    def summed(rows):
        return jnp.sum(rows.T, axis=0, keepdims=True) * scale

    def side(first):
        parts = [column[pl.ds(first + c, SIDE, stride=SIDE), :] for c in range(RIM)]
        parts.append(jnp.zeros((LANES - RIM * SIDE, LANES), F32))
        return summed(jnp.concatenate(parts, axis=0))

    top = summed(column[pl.ds(0, LANES), :])
    bottom = summed(column[pl.ds(elems - LANES, LANES), :])
    left, right = side(0), side(SIDE - RIM)
    return jnp.concatenate([top, top, top, left, right, bottom, bottom, bottom], axis=0)


def rim_places(slots, count_ref, elems):
    slots = jnp.concatenate([slots, jnp.zeros((8, LANES - slots.shape[1]), jnp.int32)], axis=1)
    lane = iota((1, LANES), 1)
    row = slots // SIDE
    col = slots - row * SIDE
    k = iota(slots.shape, 0)
    across = jnp.where(k == 3, col, col - (SIDE - RIM)) * SIDE + row
    place = jnp.where(k < 3, slots, jnp.where(k < 5, across, slots - (elems - LANES)))
    live = jnp.concatenate([jnp.where(lane < count_ref[0, d], 1.0, 0.0) for d in range(8)], axis=0)
    return jnp.where(live > 0.0, place, 0), live


def energy_kernel(
    scale, gram_any, p_hbm, dens_ref, slot_ref, count_ref, sens_ref, up_ref, down_ref, side_ref, ritz_ref,
    gram_ref, p_vmem, dcol, both, total, gram_sem, sems
):
    elems = dcol.shape[0]
    groups = elems // GROUP
    pieces = sems.shape[0]
    span = groups // pieces
    copies = [
        pltpu.make_async_copy(
            p_hbm.at[pl.ds(i * span, span)], p_vmem.at[pl.ds(i * span, span)], sems.at[i]
        )
        for i in range(pieces)
    ]
    gram_copy = pltpu.make_async_copy(gram_any, gram_ref, gram_sem)
    gram_copy.start()
    for copy in copies:
        copy.start()
    density_columns(dens_ref, dcol)
    slots, live = rim_places(slot_ref[...], count_ref, elems)
    tile_dens = jnp.take_along_axis(rims(dcol, 1.0 / LANES), slots, axis=1) * live

    gram_copy.wait()
    row, col = iota((LANES, LANES), 0), iota((LANES, LANES), 1)
    packed = gram_ref[0:LANES, :]
    above = jnp.where(row < col, packed, 0.0)
    below = jnp.where(row > col, packed, 0.0)
    stiff = above + above.T + jnp.where(row == col, packed, 0.0)
    mass = below + below.T + jnp.where(row == col, gram_ref[LANES : LANES + 1, :], 0.0)
    inv_mass = invert_spd(mass)
    ritz_ref[0, 0] = jnp.sum(inv_mass * stiff) * (1.0 / LANES)
    half = jnp.dot(inv_mass, stiff, precision=HIGHEST, preferred_element_type=F32)
    sandwich = jnp.dot(half, inv_mass, precision=HIGHEST, preferred_element_type=F32)
    both[...] = jnp.zeros_like(both)
    both[0:LANES, 0:LANES] = inv_mass.astype(BF16)
    both[LANES:, LANES:] = sandwich.astype(BF16)

    per_piece = span * GROUP // STRIP
    for i in range(pieces):
        copies[i].wait()

        def body(it, _, i=i):
            unit = i * per_piece + it
            stiffs = p_vmem[pl.ds(unit * (STRIP // GROUP), STRIP // GROUP), 0:ROWS, :].reshape(STRIP // GROUP * ROWS, LANES)
            masses = p_vmem[pl.ds(unit * (STRIP // GROUP), STRIP // GROUP), ROWS:, :].reshape(STRIP // GROUP * ROWS, LANES)
            inner = jnp.dot(
                jnp.concatenate([stiffs, masses], axis=1), both[...], preferred_element_type=F32
            )
            part_stiff = (inner[:, :LANES] * stiffs.astype(F32)).reshape(STRIP // GROUP, 24, 8, LANES).sum(axis=1)
            part_mass = (inner[:, LANES:] * masses.astype(F32)).reshape(STRIP // GROUP, 24, 8, LANES).sum(axis=1)
            at = pl.ds(pl.multiple_of(unit * STRIP, STRIP), STRIP)
            dens = dcol[at, :]
            total[at, :] = 3.0 * dens * dens * part_stiff.reshape(STRIP, LANES) - part_mass.reshape(STRIP, LANES)
            return 0

        lax.fori_loop(0, per_piece, body, 0, unroll=18)

    for j in range(elems // LANES):
        block = total[pl.ds(j * LANES, LANES), :]
        sens_ref[j : j + 1, :] = jnp.sum(block.T, axis=0, keepdims=True) * scale
    tile_sens = jnp.take_along_axis(rims(total, scale), slots, axis=1) * live
    tiles = (live, tile_dens, tile_sens)
    for ref, directions in ((up_ref, (0, 2, 1)), (down_ref, (5, 7, 6)), (side_ref, (3, 4))):
        ref[...] = jnp.zeros_like(ref)
        for n, k in enumerate(directions):
            for ch, value in enumerate(tiles):
                ref[3 * n + ch : 3 * n + ch + 1, :] = value[k : k + 1]


def project_and_gram(connectivity, block_vectors, dens_rows, stiff_factor, mass_factor):
    elems = dens_rows.size
    groups = elems // GROUP
    steps = 9
    per_step = elems // UNIT // steps
    vmem = pl.BlockSpec(memory_space=pltpu.VMEM)
    smem = pl.BlockSpec(memory_space=pltpu.SMEM)
    return pl.pallas_call(
        lambda *refs: gram_kernel(elems, per_step, *refs),
        grid=(steps,),
        out_shape=(
            jax.ShapeDtypeStruct((groups, 2 * ROWS, LANES), BF16),
            jax.ShapeDtypeStruct((LANES + 8, LANES), F32),
        ),
        in_specs=[vmem] * 5,
        out_specs=(
            pl.BlockSpec((groups // steps, 2 * ROWS, LANES), lambda i: (i, 0, 0)),
            pl.BlockSpec((LANES + 8, LANES), lambda i: (0, 0)),
        ),
        scratch_shapes=[
            pltpu.VMEM((3 * elems + 24, LANES), F32),
            pltpu.VMEM((elems, LANES), F32),
            pltpu.VMEM((2 * ROWS, ROWS), BF16),
            pltpu.VMEM((8, elems), jnp.int32),
            pltpu.SMEM((8 * elems,), jnp.int32),
            pltpu.VMEM((UNIT // 16, ROWS, 2 * LANES), BF16),
            pltpu.VMEM((UNIT // 16, ROWS, 2 * LANES), BF16),
            pltpu.VMEM((4, UNIT // GROUP, ROWS, LANES), BF16),
            pltpu.VMEM((4, UNIT // GROUP, ROWS, LANES), BF16),
            pltpu.VMEM((2, LANES, LANES), F32),
            pltpu.SemaphoreType.DMA((8,)),
        ],
        compiler_params=pltpu.CompilerParams(vmem_limit_bytes=60 * MIB),
        name="gram",
    )(connectivity, block_vectors, dens_rows, stiff_factor, mass_factor)


def energies(scale, gram, proj, dens_rows, send_slot, send_count):
    elems = dens_rows.size
    groups = elems // GROUP
    vmem = pl.BlockSpec(memory_space=pltpu.VMEM)
    smem = pl.BlockSpec(memory_space=pltpu.SMEM)
    return pl.pallas_call(
        lambda *refs: energy_kernel(scale, *refs),
        out_shape=(
            jax.ShapeDtypeStruct((elems // LANES, LANES), F32),
            jax.ShapeDtypeStruct((16, LANES), F32),
            jax.ShapeDtypeStruct((16, LANES), F32),
            jax.ShapeDtypeStruct((8, LANES), F32),
            jax.ShapeDtypeStruct((1, 1), F32),
        ),
        in_specs=[pl.BlockSpec(memory_space=pl.ANY)] * 2 + [vmem, vmem, smem],
        out_specs=(vmem,) * 4 + (smem,),
        scratch_shapes=[
            pltpu.VMEM((LANES + 8, LANES), F32),
            pltpu.VMEM((groups, 2 * ROWS, LANES), BF16),
            pltpu.VMEM((elems, LANES), F32),
            pltpu.VMEM((2 * LANES, 2 * LANES), BF16),
            pltpu.VMEM((elems, LANES), F32),
            pltpu.SemaphoreType.DMA,
            pltpu.SemaphoreType.DMA((4,)),
        ],
        compiler_params=pltpu.CompilerParams(vmem_limit_bytes=44 * MIB),
        name="energy",
    )(gram, proj, dens_rows, send_slot, send_count)


def split3(value):
    high = value.astype(BF16)
    rest = value - high.astype(F32)
    mid = rest.astype(BF16)
    low = (rest - mid.astype(F32)).astype(BF16)
    return high, mid, low


def owner_kernel(
    up_any, down_any, left_any, right_any, target_ref, weight_ref, dens_ref, sens_ref, fdens_ref, fsens_ref,
    up_ref, down_ref, left_ref, right_ref, sems
):
    pairs = ((up_any, up_ref), (down_any, down_ref), (left_any, left_ref), (right_any, right_ref))
    copies = [pltpu.make_async_copy(src, dst, sems.at[i]) for i, (src, dst) in enumerate(pairs)]
    for copy in copies:
        copy.start()
    lane = iota((1, LANES), 1)

    def lanes_of(main, corner):
        return jnp.where(lane < 96, main, pltpu.roll(corner, 96, 1))

    def by_side(table):
        table = jnp.concatenate([table, jnp.zeros((8, LANES - table.shape[1]), table.dtype)], axis=1)
        pairs = ((1, 0), (6, 5), (3, 2), (4, 7))
        return [lanes_of(table[m : m + 1], table[c : c + 1]) for m, c in pairs]

    weights = by_side(weight_ref[...])
    targets = jnp.concatenate(by_side(target_ref[...]), axis=1)
    for copy in copies:
        copy.wait()
    values = [[], [], []]
    for ch in range(3):

        def at(ref, first):
            return ref[first + ch : first + ch + 1, :]

        sides = (
            lanes_of(at(up_ref, 6), at(left_ref, 8)),
            lanes_of(at(down_ref, 6), at(left_ref, 16)),
            lanes_of(at(left_ref, 0), at(right_ref, 11)),
            lanes_of(at(right_ref, 3), at(right_ref, 19)),
        )
        for side in range(4):
            values[ch].append(sides[side] * weights[side])
    stacked = jnp.concatenate([jnp.concatenate(v, axis=1) for v in values], axis=0)
    high, mid, low = split3(stacked)
    left = jnp.concatenate([high, mid, low, jnp.zeros((7, 4 * LANES), BF16)], axis=0)
    last = dens_ref.shape[0] - 1
    for j in range(last + 1):
        part = slice(0 if j in (0, last) else 2 * LANES, 4 * LANES)
        hit = targets[:, part] == iota((LANES, part.stop - part.start), 0) + j * LANES
        hot = jnp.where(hit, 1.0, 0.0).astype(BF16)
        sums = lax.dot_general(left[:, part], hot, (((1,), (1,)), ((), ())), preferred_element_type=F32)
        sums = sums[0:3] + sums[3:6] + sums[6:9]
        under = 1.0 + sums[0:1]
        fdens_ref[j : j + 1, :] = (dens_ref[j : j + 1, :] + sums[1:2]) / under
        fsens_ref[j : j + 1, :] = (sens_ref[j : j + 1, :] + sums[2:3]) / under


def place(index, sizes):
    rows, cols = sizes
    return [index // cols // 2, index // cols % 2, index % cols // 4, index % 4]


def swapped(sizes, axis, step):
    rows, cols = sizes
    lengths = [rows // 2, 2, cols // 4, 4]
    pairs = []
    for i in range(rows * cols):
        at = place(i, sizes)
        at[axis] = (at[axis] + step) % lengths[axis]
        pairs.append((i, ((at[0] * 2 + at[1]) * lengths[2] + at[2]) * 4 + at[3]))
    return pairs


def sum_over_devices(value, sizes):
    value = value + lax.ppermute(value, AXES, swapped(sizes, 1, 1))
    lengths = [sizes[0] // 2, 2, sizes[1] // 4, 4]
    for axis in (3, 2, 0):
        others = [lax.ppermute(value, AXES, swapped(sizes, axis, s)) for s in range(1, lengths[axis])]
        for other in others:
            value = value + other
    return value


def torus(axis, step):
    size = lax.axis_size(axis)
    return [(i, (i + step) % size) for i in range(size)]


def per_device(
    block_vectors, connectivity, density, stiff_factor, mass_factor, send_slot, send_count, recv_target, recv_weight
):
    vec_count = block_vectors.shape[1]
    elems = density.shape[0]
    sizes = (lax.axis_size("gx"), lax.axis_size("gy"))
    scale = float(elems * sizes[0] * sizes[1]) / vec_count

    dens_rows = density.reshape(elems // LANES, LANES)

    proj, gram = project_and_gram(connectivity, block_vectors, dens_rows, stiff_factor, mass_factor)
    gram = sum_over_devices(gram, sizes)

    sens_rows, up, down, side, ritz = energies(scale, gram, proj, dens_rows, send_slot[0], send_count)

    up = lax.ppermute(up, "gx", torus("gx", -1))
    down = lax.ppermute(down, "gx", torus("gx", 1))
    packet = jnp.concatenate([side, up[:8], down[:8]], axis=0)
    left = lax.ppermute(packet, "gy", torus("gy", -1))
    right = lax.ppermute(packet, "gy", torus("gy", 1))

    vmem = pl.BlockSpec(memory_space=pltpu.VMEM)
    fdens, fsens = pl.pallas_call(
        owner_kernel,
        out_shape=(jax.ShapeDtypeStruct((elems // LANES, LANES), F32),) * 2,
        in_specs=[pl.BlockSpec(memory_space=pl.ANY)] * 4 + [vmem] * 4,
        out_specs=(vmem, vmem),
        scratch_shapes=[
            pltpu.VMEM((16, LANES), F32),
            pltpu.VMEM((16, LANES), F32),
            pltpu.VMEM((24, LANES), F32),
            pltpu.VMEM((24, LANES), F32),
            pltpu.SemaphoreType.DMA((4,)),
        ],
        compiler_params=pltpu.CompilerParams(vmem_limit_bytes=8 * MIB),
        name="owner",
    )(up, down, left, right, recv_target[0], recv_weight[0], dens_rows, sens_rows)
    return fdens.reshape(elems), fsens.reshape(elems), ritz.reshape(())


def solution(mesh):
    placed = (
        P(None, None, ("gx", "gy")),
        P(None, ("gx", "gy")),
        P(("gx", "gy")),
        P(),
        P(),
        P(("gx", "gy"), None, None),
        P(("gx", "gy"), None),
        P(("gx", "gy"), None, None),
        P(("gx", "gy"), None, None),
    )
    return jax.shard_map(
        per_device,
        mesh=mesh,
        in_specs=placed,
        out_specs=(P(("gx", "gy")), P(("gx", "gy")), P()),
        check_vma=False,
    )
```
